256 devices in a mesh: seq: 32 (over x, z), ch: 8 (over y, core).
Axes of the slice: x: 4, y: 4, z: 8, core: 2. Of those that a mesh axis runs over, the one named last changes fastest.
Arguments:
- signal: bfloat16 [8192, 2048], P('seq', 'ch'), may hold values from -6 to 6
- conv_taps: float32 [2, 4, 2048], P(None, None, 'ch'), may hold values from -3 to 3
- dilations: int32 [2], replicated, may hold values from 1 to 16, as said below
- decays: float32 [2, 2048], P(None, 'ch'), may hold values from 0.96 to 1
- retention: float32 [8192], P('seq'), may hold values from 0.5 to 1
- readout: float32 [2, 2048], P(None, 'ch'), may hold values from -4 to 4
- skip_gain: float32 [2048], P('ch'), may hold values from 0.5 to 1.5
- w_out: bfloat16 [2048, 2048], P('ch'), may hold values from -0.125 to 0.125
- cotangent: bfloat16 [8192, 2048], P('seq', 'ch'), may hold values from -6 to 6
Outputs:
- output: bfloat16 [8192, 2048], P('seq', 'ch')
- grad_signal: bfloat16 [8192, 2048], P('seq', 'ch')
- grad_w_out: float32 [2048, 2048], P('ch', 'seq')
The draws below stay inside these ranges and needn't reach their ends.
Inputs may be any that keep to these rules, and one draw needn't show every extreme that they name: `dilations`: one of the two equals 16, the other is smaller.
All inputs are finite; a program needn't handle non-finite values.
Results may differ from the reference program's by a relative error of at most 0.0042.
Values may be sent and summed in bfloat16 or wider, within the bound.
No kernel may reach another device: no remote copies, remote signals or barrier semaphores. Data moves between devices by JAX's collectives and lax.ppermute only.
A program may use at most 64 MiB of HBM per device.

```python
import math
import jax
import jax.numpy as jnp
from jax import lax

D = 2048
K = 4
DMAX = 16
TOKENS = 8192


def draw_dilations(key, part):
    key = jax.random.fold_in(key, 11)
    first_key, second_key = jax.random.split(key)
    chosen = jax.random.randint(first_key, (), 0, 2)
    others = jax.random.randint(second_key, (2,), 1, DMAX)
    return jnp.where(jnp.arange(2) == chosen, DMAX, others).astype(jnp.int32)


def draw_decays(key, part):
    key = jax.random.fold_in(key, 23)
    first_key, second_key = jax.random.split(key)
    share = 0.5
    slower = jax.random.bernoulli(first_key, share, (2, D))
    spread = jax.random.uniform(second_key, (2, D), jnp.float32)
    lowest = math.log(0.1 / TOKENS)
    middle = math.log(1.0 / TOKENS)
    highest = math.log(1.0 / 30.0)
    rates = jnp.where(slower, lowest + spread * (middle - lowest), middle + spread * (highest - middle))
    return (1.0 - jnp.exp(rates)).astype(jnp.float32)


def draw_retention(key, part):
    key = jax.random.fold_in(key, 37)
    first_key, second_key = jax.random.split(key)
    places = jax.random.randint(first_key, (3,), 0, TOKENS)
    levels = jax.random.uniform(second_key, (3,), jnp.float32, 0.5, 0.8)
    steps = jnp.arange(TOKENS)
    struck = steps[:, None] == places[None, :]
    return jnp.prod(jnp.where(struck, levels[None, :], 1.0), axis=1).astype(jnp.float32)


def strengthened(result, stream_key, source, target, blocks, factor):
    def block_of(position):
        return (jnp.arange(result.shape[position]) // (result.shape[position] // blocks)).reshape((-1,) + (1,) * (result.ndim - 1 - position))

    first = jax.random.permutation(stream_key, blocks)[block_of(target)]
    other_side = (block_of(target) + blocks // 2) % blocks
    return jnp.where((block_of(source) == first) | (block_of(source) == other_side), factor * result, result)


def shard_levels(rng, extent, shards, least, largest):
    def one(axis_at, blocks):
        steps = jax.random.uniform(jax.random.fold_in(jax.random.fold_in(rng, 6), axis_at), (blocks,), jnp.float32, least / len(shards), largest / len(shards))
        return jnp.repeat(jnp.exp(steps), extent[axis_at] // blocks).reshape((-1,) + (1,) * (len(extent) - axis_at - 1))

    gain = one(*shards[0])
    for cut in shards[1:]:
        gain = gain * one(*cut)
    return gain


def centred(own_key, extent, scale, reach, cuts=(), dtype=jnp.bfloat16):
    loudness = shard_levels(own_key, extent, cuts, -0.22, 0.18) if cuts else 1.0
    array = jax.random.normal(own_key, extent, jnp.float32) * scale * loudness
    return jnp.minimum(jnp.maximum(array, -reach), reach).astype(dtype)


def bell_draw_with(stream_key, shape, width, bound, pieces, heavy, dtype=jnp.bfloat16):
    values = width * jax.random.normal(stream_key, shape, jnp.float32)
    if pieces:
        values = values * shard_levels(stream_key, shape, pieces, -0.22, 0.18)
    return jnp.clip(strengthened(values, jax.random.fold_in(stream_key, 3), *heavy), -bound, bound).astype(dtype)


def setup_inputs(seed: int = 0) -> dict:
    arg_keys = jax.random.split(jax.random.key(seed), 10)
    signal = centred(arg_keys[0], (TOKENS, D), 1.0, 6.0, ((0, 32), (1, 8)))
    conv_taps = centred(arg_keys[1], (2, K, D), K ** -0.5, 3.0, ((2, 8),), jnp.float32)
    dilations = draw_dilations(jax.random.fold_in(arg_keys[9], 71), 0)
    decays = draw_decays(jax.random.fold_in(arg_keys[9], 71), 0)
    retention = draw_retention(jax.random.fold_in(arg_keys[9], 71), 0)
    readout = centred(arg_keys[5], (2, D), 1.0, 4.0, ((1, 8),), jnp.float32)
    skip_gain = jnp.clip(0.5 + 1.0 * jax.random.uniform(arg_keys[6], (D,), jnp.float32) ** shard_levels(arg_keys[6], (D,), ((0, 8),), -0.2, 0.2), 0.5, 1.5)
    w_out = centred(arg_keys[7], (D, D), D ** -0.5, 0.125, ((0, 8),))
    cotangent = bell_draw_with(arg_keys[8], (TOKENS, D), 1.0, 6.0, ((0, 32), (1, 8)), (0, 1, 32, 2.75))
    return dict(signal=signal, conv_taps=conv_taps, dilations=dilations, decays=decays, retention=retention, readout=readout, skip_gain=skip_gain, w_out=w_out, cotangent=cotangent)


def combine(earlier, later):
    return (earlier[0] * later[0], later[0] * earlier[1] + later[1])

def causal_conv(values, weights, spacing):
    length = values.shape[0]
    margin = (K - 1) * DMAX
    padded = jnp.pad(values, ((margin, 0), (0, 0)))
    total = jnp.zeros(values.shape, jnp.float32)
    for lag_index in range(K):
        total = total + weights[lag_index] * lax.dynamic_slice_in_dim(padded, margin - lag_index * spacing, length, 0)
    return total

def later_conv(values, weights, spacing):
    length = values.shape[0]
    margin = (K - 1) * DMAX
    padded = jnp.pad(values, ((0, margin), (0, 0)))
    total = jnp.zeros(values.shape, jnp.float32)
    for lag_index in range(K):
        total = total + weights[lag_index] * lax.dynamic_slice_in_dim(padded, lag_index * spacing, length, 0)
    return total

def reference(signal, conv_taps, dilations, decays, retention, readout, skip_gain, w_out, cotangent):
    widened = signal.astype(jnp.float32)
    first = causal_conv(widened, conv_taps[0], dilations[0])
    driven = causal_conv(first, conv_taps[1], dilations[1])
    gamma = jnp.sqrt(1.0 - decays * decays)
    factor = decays[None, :, :] * retention[:, None, None]
    inputs = gamma[None, :, :] * driven[:, None, :]
    _, state = lax.associative_scan(combine, (factor, inputs), axis=0)
    mixed = (readout[0] * state[:, 0, :] + readout[1] * state[:, 1, :] + skip_gain * driven).astype(jnp.bfloat16)
    output = (widened + jnp.dot(mixed, w_out, preferred_element_type=jnp.float32)).astype(jnp.bfloat16)
    grad_mixed = lax.dot_general(cotangent, w_out, (((1,), (1,)), ((), ())), preferred_element_type=jnp.float32)
    grad_w_out = lax.dot_general(mixed, cotangent, (((0,), (0,)), ((), ())), preferred_element_type=jnp.float32)
    emitted = readout[None, :, :] * grad_mixed[:, None, :]
    _, passed = lax.associative_scan(combine, (factor, factor * emitted), axis=0, reverse=True)
    following = jnp.concatenate([passed[1:], jnp.zeros((1,) + passed.shape[1:], jnp.float32)], axis=0)
    grad_state = emitted + following
    grad_driven = skip_gain * grad_mixed + (gamma[0] * grad_state[:, 0, :] + gamma[1] * grad_state[:, 1, :])
    grad_first = later_conv(grad_driven, conv_taps[1], dilations[1])
    grad_branch = later_conv(grad_first, conv_taps[0], dilations[0])
    grad_signal = (cotangent.astype(jnp.float32) + grad_branch).astype(jnp.bfloat16)
    return (output, grad_signal, grad_w_out)
```

```python
import functools
import jax
import jax.numpy as jnp
from jax import lax
from jax.experimental import pallas as pl
from jax.experimental.pallas import tpu as pltpu
from jax.sharding import PartitionSpec as P

K = 4
DMAX = 16
MARGIN = (K - 1) * DMAX
REACH = 2 * MARGIN
SEGS = 8
LANES = 128
ZSIZE = 8
F32 = jnp.float32
BF16 = jnp.bfloat16


def spread_rows(row):
    return jnp.transpose(jnp.broadcast_to(row, (LANES, row.shape[1])))


def row_of(value, index):
    return value[index : index + 1]


def power(value, exponent):
    while exponent > 1:
        value = value * value
        exponent //= 2
    return value


def halves(count):
    return [(half, slice(half * LANES, (half + 1) * LANES)) for half in range(count // LANES)]


def lanes_of(ref, which, cols):
    return ref[which : which + 1, cols]


def fill_copies(pay_ref, rows):
    tile = jnp.concatenate(rows, axis=0)
    for copy in range(pay_ref.shape[0] // 8):
        pay_ref[8 * copy : 8 * copy + 8, :] = tile


def forward_local(
    dil_ref, halo_ref, sig_ref, taps_ref, dec_ref, ret_ref,
    drv_ref, pay_ref, segh_ref, segp_ref,
    ext_ref, first_ref, rb_ref,
):
    rows, width = sig_ref.shape
    steps = rows // SEGS
    rb_ref[...] = spread_rows(ret_ref[...])
    ends = [[None] * 2 for _ in range(2)]
    prods = [[None] * 2 for _ in range(2)]
    for half, cols in halves(width):
        ext_ref[0:REACH, :] = halo_ref[:, cols].astype(F32)
        ext_ref[REACH : REACH + rows, :] = sig_ref[:, cols].astype(F32)
        total = jnp.zeros((rows + MARGIN, LANES), F32)
        for k in range(K):
            total = total + taps_ref[0, k : k + 1, cols] * ext_ref[
                pl.ds(MARGIN - k * dil_ref[0], rows + MARGIN), :
            ]
        first_ref[...] = total
        total = jnp.zeros((rows, LANES), F32)
        for k in range(K):
            total = total + taps_ref[1, k : k + 1, cols] * first_ref[
                pl.ds(MARGIN - k * dil_ref[1], rows), :
            ]
        drv_ref[half] = total
        decay = [lanes_of(dec_ref, p, cols) for p in range(2)]
        gamma = [jnp.sqrt(1.0 - d * d) for d in decay]
        state = [jnp.zeros((SEGS, LANES), F32) for _ in range(2)]
        kept = jnp.ones((SEGS, LANES), F32)
        for i in range(steps):
            r = rb_ref[pl.ds(i, SEGS, stride=steps), :]
            u = drv_ref[half, pl.ds(i, SEGS, stride=steps), :]
            kept = kept * r
            for p in range(2):
                state[p] = (decay[p] * r) * state[p] + gamma[p] * u
        for p in range(2):
            seg = kept * power(decay[p], steps)
            segh_ref[half, p] = state[p]
            segp_ref[half, p] = seg
            end = row_of(state[p], 0)
            prod = row_of(seg, 0)
            for s in range(1, SEGS):
                end = row_of(seg, s) * end + row_of(state[p], s)
                prod = prod * row_of(seg, s)
            ends[p][half] = end
            prods[p][half] = prod
    fill_copies(pay_ref, ends[0] + ends[1] + prods[0] + prods[1])


def forward_final(
    me_ref, got_ref, drv_ref, segh_ref, segp_ref, dec_ref, ret_ref, ro_ref, skip_ref, cot_ref,
    mixed_ref, w0_ref, w1_ref, w2_ref, w3_ref,
    rb_ref, mix_ref,
):
    rows, width = mixed_ref.shape
    steps = rows // SEGS
    me = me_ref[0]
    count = got_ref.shape[0] // 8
    rb_ref[...] = spread_rows(ret_ref[...])
    entering = jnp.zeros((4, LANES), F32)
    for i in range(count - 1):
        longer = got_ref[8 * i + 4 : 8 * i + 8, :] * entering + got_ref[8 * i : 8 * i + 4, :]
        entering = jnp.where(i < me, longer, entering)
    for half, cols in halves(width):
        decay = [lanes_of(dec_ref, p, cols) for p in range(2)]
        gamma = [jnp.sqrt(1.0 - d * d) for d in decay]
        readout = [lanes_of(ro_ref, p, cols) for p in range(2)]
        skip = skip_ref[0:1, cols]
        state = []
        for p in range(2):
            here = row_of(entering, 2 * p + half)
            starts = [here]
            for s in range(SEGS - 1):
                here = segp_ref[half, p, s : s + 1, :] * here + segh_ref[half, p, s : s + 1, :]
                starts.append(here)
            state.append(jnp.concatenate(starts, axis=0))
        for i in range(steps):
            r = rb_ref[pl.ds(i, SEGS, stride=steps), :]
            u = drv_ref[half, pl.ds(i, SEGS, stride=steps), :]
            for p in range(2):
                state[p] = (decay[p] * r) * state[p] + gamma[p] * u
            mix_ref[half, pl.ds(i, SEGS, stride=steps), :] = (
                readout[0] * state[0] + readout[1] * state[1] + skip * u
            )
        mixed_ref[:, cols] = mix_ref[half].astype(BF16)
    flipped = jnp.transpose(
        jnp.concatenate([mix_ref[half] for half, _ in halves(width)], axis=1)
    ).astype(BF16)
    parts = (w0_ref, w1_ref, w2_ref, w3_ref)
    block = cot_ref.shape[1] // 4
    for d, part in enumerate(parts):
        start = pl.multiple_of(lax.rem(me // ZSIZE + d, 4) * block, block)
        part[...] = jnp.dot(
            flipped, cot_ref[:, pl.ds(start, block)], preferred_element_type=F32
        ).astype(part.dtype)


def backward_local(
    cot_ref, wout_ref, segp_ref, dec_ref, ret_ref, ro_ref, skip_ref,
    gm_ref, pay_ref, segw_ref, halo_ref,
    rb_ref, gd_ref,
):
    rows = cot_ref.shape[0]
    width = wout_ref.shape[0]
    steps = rows // SEGS
    rb_ref[...] = spread_rows(ret_ref[...])
    grad_mixed = lax.dot_general(
        cot_ref[...], wout_ref[...], (((1,), (1,)), ((), ())), preferred_element_type=F32
    )
    ends = [[None] * 2 for _ in range(2)]
    prods = [[None] * 2 for _ in range(2)]
    for half, cols in halves(width):
        gm_ref[half] = grad_mixed[:, cols]
        decay = [lanes_of(dec_ref, p, cols) for p in range(2)]
        gamma = [jnp.sqrt(1.0 - d * d) for d in decay]
        readout = [lanes_of(ro_ref, p, cols) for p in range(2)]
        skip = skip_ref[0:1, cols]
        passed = [jnp.zeros((SEGS, LANES), F32) for _ in range(2)]
        for i in reversed(range(steps)):
            r = rb_ref[pl.ds(i, SEGS, stride=steps), :]
            g = gm_ref[half, pl.ds(i, SEGS, stride=steps), :]
            for p in range(2):
                passed[p] = (decay[p] * r) * (readout[p] * g + passed[p])
        inits = []
        for p in range(2):
            segw_ref[half, p] = passed[p]
            here = jnp.zeros((1, LANES), F32)
            starts = [here]
            prod = segp_ref[half, p, 0:1, :]
            for s in reversed(range(1, SEGS)):
                here = row_of(passed[p], s) + segp_ref[half, p, s : s + 1, :] * here
                prod = prod * segp_ref[half, p, s : s + 1, :]
                starts.append(here)
            ends[p][half] = row_of(passed[p], 0) + segp_ref[half, p, 0:1, :] * here
            prods[p][half] = prod
            inits.append(jnp.concatenate(starts[::-1], axis=0))
        for i in reversed(range(steps)):
            r = rb_ref[pl.ds(i, SEGS, stride=steps), :]
            g = gm_ref[half, pl.ds(i, SEGS, stride=steps), :]
            total = None
            for p in range(2):
                grad_state = readout[p] * g + inits[p]
                inits[p] = (decay[p] * r) * grad_state
                term = gamma[p] * grad_state
                total = term if total is None else total + term
            gd_ref[pl.ds(i, SEGS, stride=steps), :] = skip * g + total
        halo_ref[:, cols] = gd_ref[0:REACH, :].astype(BF16)
    fill_copies(pay_ref, ends[0] + ends[1] + prods[0] + prods[1])


def backward_final(
    me_ref, dil_ref, got_ref, gm_ref, segw_ref, segp_ref, halo_ref, ret_ref, next_ref,
    dec_ref, ro_ref, skip_ref, taps_ref, cot_ref,
    out_ref,
    rb_ref, rn_ref, ahead_ref, far_ref, first_ref,
):
    rows, width = cot_ref.shape
    steps = rows // SEGS
    me = me_ref[0]
    count = got_ref.shape[0] // 8
    rb_ref[...] = spread_rows(ret_ref[...])
    rn_ref[...] = spread_rows(next_ref[...])
    arriving = jnp.zeros((4, LANES), F32)
    beyond = jnp.zeros((4, LANES), F32)
    for i in reversed(range(1, count)):
        prod = got_ref[8 * i + 4 : 8 * i + 8, :]
        own = got_ref[8 * i : 8 * i + 4, :]
        longer = prod * arriving + own
        beyond = jnp.where(i > me + 1, longer, beyond)
        arriving = jnp.where(i > me, longer, arriving)
    kept = jnp.ones((SEGS, LANES), F32)
    for i in range(steps):
        kept = kept * rn_ref[pl.ds(i, SEGS, stride=steps), :]
    for half, cols in halves(width):
        decay = [lanes_of(dec_ref, p, cols) for p in range(2)]
        gamma = [jnp.sqrt(1.0 - d * d) for d in decay]
        readout = [lanes_of(ro_ref, p, cols) for p in range(2)]
        skip = skip_ref[0:1, cols]
        here_at, far_at = [], []
        for p in range(2):
            here = row_of(arriving, 2 * p + half)
            far = row_of(beyond, 2 * p + half)
            seg = kept * power(decay[p], steps)
            starts, fars = [here], [far]
            for s in reversed(range(1, SEGS)):
                here = segw_ref[half, p, s : s + 1, :] + segp_ref[half, p, s : s + 1, :] * here
                far = row_of(seg, s) * far
                starts.append(here)
                fars.append(far)
            here_at.append(jnp.concatenate(starts[::-1], axis=0))
            far_at.append(jnp.concatenate(fars[::-1], axis=0))
        for i in reversed(range(steps)):
            r = rb_ref[pl.ds(i, SEGS, stride=steps), :]
            rn = rn_ref[pl.ds(i, SEGS, stride=steps), :]
            g = gm_ref[half, pl.ds(i, SEGS, stride=steps), :]
            total = far_total = None
            for p in range(2):
                grad_state = readout[p] * g + here_at[p]
                here_at[p] = (decay[p] * r) * grad_state
                term = gamma[p] * grad_state
                total = term if total is None else total + term
                term = gamma[p] * far_at[p]
                far_total = term if far_total is None else far_total + term
                far_at[p] = (decay[p] * rn) * far_at[p]
            ahead_ref[pl.ds(i, SEGS, stride=steps), :] = skip * g + total
            far_ref[pl.ds(i, SEGS, stride=steps), :] = far_total
        ahead_ref[rows : rows + REACH, :] = halo_ref[:, cols].astype(F32) + far_ref[0:REACH, :]
        total = jnp.zeros((rows + MARGIN, LANES), F32)
        for k in range(K):
            total = total + taps_ref[1, k : k + 1, cols] * ahead_ref[
                pl.ds(k * dil_ref[1], rows + MARGIN), :
            ]
        first_ref[...] = total
        total = jnp.zeros((rows, LANES), F32)
        for k in range(K):
            total = total + taps_ref[0, k : k + 1, cols] * first_ref[pl.ds(k * dil_ref[0], rows), :]
        out_ref[:, cols] = (cot_ref[:, cols].astype(F32) + total).astype(BF16)


def near_sum(a_ref, b_ref, c_ref, d_ref, out_ref):
    total = (a_ref[...].astype(F32) + b_ref[...].astype(F32)) + (
        c_ref[...].astype(F32) + d_ref[...].astype(F32)
    )
    rows, width = total.shape
    wide = width // ZSIZE
    for z in range(ZSIZE):
        piece = total[:, z * wide : (z + 1) * wide]
        out_ref[z] = jnp.concatenate([piece[: rows // 2], piece[rows // 2 :]], axis=1).astype(BF16)


def far_sum(in_ref, out_ref):
    total = in_ref[0].astype(F32)
    for z in range(1, ZSIZE):
        total = total + in_ref[z].astype(F32)
    wide = total.shape[1] // 2
    out_ref[...] = jnp.concatenate([total[:, :wide], total[:, wide:]], axis=0)


def call(kernel, outs, smem, scratch, name):
    def run(*args):
        specs = [
            pl.BlockSpec(memory_space=pltpu.SMEM if i < smem else pltpu.VMEM)
            for i in range(len(args))
        ]
        return pl.pallas_call(
            kernel,
            out_shape=tuple(jax.ShapeDtypeStruct(shape, dtype) for shape, dtype in outs),
            in_specs=specs,
            out_specs=tuple(pl.BlockSpec(memory_space=pltpu.VMEM) for _ in outs),
            scratch_shapes=[pltpu.VMEM(shape, F32) for shape in scratch],
            compiler_params=pltpu.CompilerParams(vmem_limit_bytes=40 * 2**20),
            name=name,
        )(*args)

    return run


def shifted(block, distance):
    devices = range(lax.axis_size("seq"))
    return lax.ppermute(
        block, "seq", [(i - distance, i) for i in devices if i - distance in devices]
    )


def along_x(block, distance):
    size = lax.axis_size("seq")
    return lax.ppermute(
        block, "seq", [(i, (i + distance * ZSIZE) % size) for i in range(size)]
    )


def per_device(
    signal, conv_taps, dilations, decays, retention, readout, skip_gain, w_out, cotangent
):
    rows, width = signal.shape
    count = lax.axis_size("seq")
    xsize = count // ZSIZE
    me = lax.axis_index("seq").astype(jnp.int32).reshape(1)
    ret = retention.reshape(1, rows)
    skip = skip_gain.reshape(1, width)
    nh = width // LANES

    halo = shifted(signal[rows - REACH :], 1)
    ret_next = shifted(ret, -1)
    all_cot = lax.all_gather(cotangent, "ch", axis=1, tiled=True)

    seg = ((nh, 2, SEGS, LANES), F32)
    tall = ((nh, rows, LANES), F32)
    pay = ((count * 8, LANES), F32)
    driven, payload, segh, segp = call(
        forward_local, [tall, pay, seg, seg], 1,
        [(rows + REACH, LANES), (rows + MARGIN, LANES), (rows, LANES)], "forward_local",
    )(dilations, halo, signal, conv_taps, decays, ret)
    got = lax.all_to_all(payload, "seq", 0, 0, tiled=True)

    block = all_cot.shape[1] // xsize
    mixed, w0, w1, w2, w3 = call(
        forward_final, [((rows, width), BF16)] + [((width, block), BF16)] * 4, 1,
        [(rows, LANES), (nh, rows, LANES)], "forward_final",
    )(me, got, driven, segh, segp, decays, ret, readout, skip, all_cot)
    w1, w2, w3 = along_x(w1, 1), along_x(w2, 2), along_x(w3, 3)

    partial = jnp.dot(mixed, w_out, preferred_element_type=F32)
    projected = lax.psum_scatter(partial, "ch", scatter_dimension=1, tiled=True)
    output = (signal.astype(F32) + projected).astype(BF16)

    grad_mixed, bpay, segw, bhalo = call(
        backward_local, [tall, pay, seg, ((REACH, width), BF16)], 0,
        [(rows, LANES), (rows, LANES)], "backward_local",
    )(all_cot, w_out, segp, decays, ret, readout, skip)
    later = shifted(bhalo, -1)
    bgot = lax.all_to_all(bpay, "seq", 0, 0, tiled=True)

    groups = [[x * ZSIZE + z for z in range(ZSIZE)] for x in range(xsize)]
    wide = block // ZSIZE
    (near,) = call(near_sum, [((ZSIZE, width // 2, 2 * wide), BF16)], 0, [], "near_sum")(
        w0, w1, w2, w3
    )
    far = lax.all_to_all(near, "seq", 0, 0, axis_index_groups=groups, tiled=True)
    (grad_w_out,) = call(far_sum, [((width, wide), F32)], 0, [], "far_sum")(far)

    (grad_signal,) = call(
        backward_final, [((rows, width), BF16)], 2,
        [(rows, LANES), (rows, LANES), (rows + REACH, LANES), (rows, LANES), (rows + MARGIN, LANES)],
        "backward_final",
    )(
        me, dilations, bgot, grad_mixed, segw, segp, later, ret, ret_next,
        decays, readout, skip, conv_taps, cotangent,
    )
    return (output, grad_signal, grad_w_out)


def solution(mesh):
    return jax.shard_map(
        per_device,
        mesh=mesh,
        in_specs=(
            P("seq", "ch"),
            P(None, None, "ch"),
            P(),
            P(None, "ch"),
            P("seq"),
            P(None, "ch"),
            P("ch"),
            P("ch", None),
            P("seq", "ch"),
        ),
        out_specs=(P("seq", "ch"), P("seq", "ch"), P("ch", "seq")),
        check_vma=False,
    )
```

```python
import jax
import jax.numpy as jnp
from jax import lax
from jax.experimental import pallas as pl
from jax.experimental.pallas import tpu as pltpu
from jax.sharding import PartitionSpec as P

K = 4
DMAX = 16
MARGIN = (K - 1) * DMAX
REACH = 2 * MARGIN
SEGS = 8
LANES = 128
XSIZE, YSIZE, ZSIZE = 4, 4, 8
F32 = jnp.float32
BF16 = jnp.bfloat16
DECAY, GAMMA, READ, SKIP, DIL, PARAMS = 8, 10, 12, 14, 15, 16


def spread_rows(row):
    return jnp.transpose(jnp.broadcast_to(row, (LANES, row.shape[1])))


def row_of(value, index):
    return value[index : index + 1]


def power(value, exponent):
    while exponent > 1:
        value = value * value
        exponent //= 2
    return value


def halves(count):
    return [(half, slice(half * LANES, (half + 1) * LANES)) for half in range(count // LANES)]


def params(par_ref, first, cols):
    return [par_ref[first + p : first + p + 1, cols] for p in range(2)]


def dilation(par_ref, which):
    return jnp.max(par_ref[DIL : DIL + 1, which * LANES : (which + 1) * LANES]).astype(jnp.int32)


def x_index():
    return lax.axis_index("seq") // ZSIZE


def y_index():
    return lax.axis_index("ch") // 2


def core_index():
    return lax.rem(lax.axis_index("ch"), 2)


def gather_inputs(
    sig_hbm, taps_hbm, dec_hbm, ret_hbm, ro_hbm, skip_hbm, cot_hbm, dil_hbm,
    par_ref, rb_ref, drv_ref, fhead_ref, shead_ref, cot_ref,
    sig_ref, taps_ref, dec_ref, ret_ref, ro_ref, skip_ref, dil_ref, ext_ref, first_ref, sems,
):
    pairs = (
        (sig_hbm, sig_ref), (taps_hbm, taps_ref), (dec_hbm, dec_ref),
        (ret_hbm, ret_ref), (ro_hbm, ro_ref), (skip_hbm, skip_ref), (cot_hbm, cot_ref),
        (dil_hbm, dil_ref),
    )
    copies = [pltpu.make_async_copy(a, b, sems.at[i]) for i, (a, b) in enumerate(pairs)]
    for copy in copies:
        copy.start()
    for copy in copies:
        copy.wait()
    rows, width = sig_ref.shape
    par_ref[0:K, :] = taps_ref[0]
    par_ref[K : 2 * K, :] = taps_ref[1]
    decays = dec_ref[...]
    par_ref[DECAY : DECAY + 2, :] = decays
    par_ref[GAMMA : GAMMA + 2, :] = jnp.sqrt(1.0 - decays * decays)
    par_ref[READ : READ + 2, :] = ro_ref[...]
    par_ref[SKIP : SKIP + 1, :] = skip_ref[...]
    for which in range(2):
        par_ref[DIL : DIL + 1, which * LANES : (which + 1) * LANES] = jnp.full(
            (1, LANES), dil_ref[which], jnp.int32
        ).astype(F32)
    rb_ref[...] = spread_rows(ret_ref[...])
    for half, cols in halves(width):
        ext_ref[...] = sig_ref[:, cols].astype(F32)
        shead_ref[half] = ext_ref[0:MARGIN, :]
        total = jnp.zeros((rows - MARGIN, LANES), F32)
        for k in range(K):
            total = total + taps_ref[0, k : k + 1, cols] * ext_ref[
                pl.ds(MARGIN - k * dil_ref[0], rows - MARGIN), :
            ]
        first_ref[...] = total
        fhead_ref[half] = first_ref[0:MARGIN, :]
        total = jnp.zeros((rows - REACH, LANES), F32)
        for k in range(K):
            total = total + taps_ref[1, k : k + 1, cols] * first_ref[
                pl.ds(MARGIN - k * dil_ref[1], rows - REACH), :
            ]
        drv_ref[half, 0:REACH, :] = jnp.zeros((REACH, LANES), F32)
        drv_ref[half, REACH:rows, :] = total


def forward_local(
    halo_ref, par_ref, rb_ref, drvin_ref, fhead_ref, shead_ref,
    drv_ref, ends_ref, segh_ref, segp_ref,
    ext_ref, first_ref,
):
    rows = rb_ref.shape[0]
    width = par_ref.shape[1]
    steps = rows // SEGS
    first_gap, second_gap = dilation(par_ref, 0), dilation(par_ref, 1)
    for half, cols in halves(width):
        ext_ref[0:REACH, :] = halo_ref[:, cols].astype(F32)
        ext_ref[REACH : REACH + MARGIN, :] = shead_ref[half]
        total = jnp.zeros((REACH, LANES), F32)
        for k in range(K):
            total = total + par_ref[k : k + 1, cols] * ext_ref[
                pl.ds(MARGIN - k * first_gap, REACH), :
            ]
        first_ref[0:REACH, :] = total
        first_ref[REACH : REACH + MARGIN, :] = fhead_ref[half]
        total = jnp.zeros((REACH, LANES), F32)
        for k in range(K):
            total = total + par_ref[K + k : K + k + 1, cols] * first_ref[
                pl.ds(MARGIN - k * second_gap, REACH), :
            ]
        drv_ref[half, 0:REACH, :] = total
        decay, gamma = params(par_ref, DECAY, cols), params(par_ref, GAMMA, cols)
        state = [jnp.zeros((SEGS, LANES), F32) for _ in range(2)]
        kept = jnp.ones((SEGS, LANES), F32)
        for i in range(steps):
            r = rb_ref[pl.ds(i, SEGS, stride=steps), :]
            u = drv_ref[half, pl.ds(i, SEGS, stride=steps), :]
            kept = kept * r
            for p in range(2):
                state[p] = (decay[p] * r) * state[p] + gamma[p] * u
        for p in range(2):
            seg = kept * power(decay[p], steps)
            segh_ref[half, p] = state[p]
            segp_ref[half, p] = seg
            end = row_of(state[p], 0)
            for s in range(1, SEGS):
                end = row_of(seg, s) * end + row_of(state[p], s)
            ends_ref[2 * p + half : 2 * p + half + 1, :] = end


def decays_of(par_ref, rows):
    parts = [par_ref[DECAY + p : DECAY + p + 1, cols] for p in range(2) for _, cols in halves(2 * LANES)]
    return power(jnp.concatenate(parts, axis=0), rows)


def forward_final(
    got_ref, drv_ref, segh_ref, segp_ref, par_ref, rb_ref, near_ref, far_ref,
    mixed_ref, w0_ref, w1_ref, w2_ref, w3_ref, rprod_ref,
    mix_ref,
):
    rows, width = mixed_ref.shape
    steps = rows // SEGS
    me = lax.axis_index("seq")
    count = got_ref.shape[0]
    kept = jnp.concatenate(
        [got_ref[i, 2, 0:1, :] * got_ref[i, 2, 1:2, :] for i in range(count)], axis=0
    )
    gap = LANES // 2
    while gap:
        kept = kept * pltpu.roll(kept, gap, axis=1)
        gap //= 2
    rprod_ref[...] = kept
    whole = decays_of(par_ref, rows)
    entering = jnp.zeros((4, LANES), F32)
    for i in range(count - 1):
        longer = (whole * rprod_ref[i : i + 1, :]) * entering + got_ref[i, 0]
        entering = jnp.where(i < me, longer, entering)
    for half, cols in halves(width):
        decay, gamma = params(par_ref, DECAY, cols), params(par_ref, GAMMA, cols)
        readout = params(par_ref, READ, cols)
        skip = par_ref[SKIP : SKIP + 1, cols]
        state = []
        for p in range(2):
            here = row_of(entering, 2 * p + half)
            starts = [here]
            for s in range(SEGS - 1):
                here = segp_ref[half, p, s : s + 1, :] * here + segh_ref[half, p, s : s + 1, :]
                starts.append(here)
            state.append(jnp.concatenate(starts, axis=0))
        for i in range(steps):
            r = rb_ref[pl.ds(i, SEGS, stride=steps), :]
            u = drv_ref[half, pl.ds(i, SEGS, stride=steps), :]
            for p in range(2):
                state[p] = (decay[p] * r) * state[p] + gamma[p] * u
            mix_ref[half, pl.ds(i, SEGS, stride=steps), :] = (
                readout[0] * state[0] + readout[1] * state[1] + skip * u
            )
        mixed_ref[:, cols] = mix_ref[half].astype(BF16)
    flipped = jnp.transpose(
        jnp.concatenate([mix_ref[half] for half, _ in halves(width)], axis=1)
    ).astype(BF16)
    core = core_index()
    mine = pl.ds(pl.multiple_of(core * width, width), width)
    other = pl.ds(pl.multiple_of((1 - core) * width, width), width)
    for d, part in ((1, w1_ref), (2, w2_ref), (3, w3_ref), (0, w0_ref)):
        at = lax.rem(y_index() - x_index() - d + 2 * YSIZE, YSIZE)
        for cols, source in ((mine, near_ref), (other, far_ref)):
            part[:, cols] = jnp.dot(
                flipped, source[at], preferred_element_type=F32
            ).astype(part.dtype)


def project(mixed_ref, wout_ref, send_ref):
    width = mixed_ref.shape[1]
    for d in range(YSIZE):
        block = 2 * lax.rem(y_index() + d, YSIZE) + 1 - core_index()
        start = pl.multiple_of(block * width, width)
        send_ref[d] = jnp.dot(
            mixed_ref[...], wout_ref[:, pl.ds(start, width)], preferred_element_type=F32
        ).astype(BF16)


def pair_sum(mixed_ref, wout_ref, got_ref, own_ref, a_ref, b_ref, c_ref):
    width = mixed_ref.shape[1]
    for d, out_ref in ((1, a_ref), (2, b_ref), (3, c_ref), (0, own_ref)):
        block = 2 * lax.rem(y_index() + d, YSIZE) + core_index()
        start = pl.multiple_of(block * width, width)
        total = got_ref[d].astype(F32) + jnp.dot(
            mixed_ref[...], wout_ref[:, pl.ds(start, width)], preferred_element_type=F32
        )
        out_ref[...] = total.astype(out_ref.dtype)


def finish_output(sig_ref, own_ref, a_ref, b_ref, c_ref, out_ref):
    total = (own_ref[...] + a_ref[...].astype(F32)) + (
        b_ref[...].astype(F32) + c_ref[...].astype(F32)
    )
    out_ref[...] = (sig_ref[...].astype(F32) + total).astype(BF16)


def pack(own_ref, a_ref, b_ref, c_ref, out_ref):
    for d, source in enumerate((own_ref, a_ref, b_ref, c_ref)):
        out_ref[d] = source[...]


def backward_local(
    near_ref, far_ref, wout_ref, segp_ref, par_ref, rb_ref, ends_ref, ret_ref,
    gm_ref, pay_ref, segw_ref, halo_ref,
    gd_ref, tile_ref,
):
    rows = rb_ref.shape[0]
    width = par_ref.shape[1]
    steps = rows // SEGS
    core = core_index()
    grad_mixed = jnp.zeros((rows, width), F32)
    for source, which in ((near_ref, core), (far_ref, 1 - core)):
        for d in range(YSIZE):
            first = 2 * lax.rem(y_index() - d + YSIZE, YSIZE)
            start = pl.multiple_of((first + which) * width, width)
            grad_mixed = grad_mixed + lax.dot_general(
                source[d], wout_ref[:, pl.ds(start, width)], (((1,), (1,)), ((), ())),
                preferred_element_type=F32,
            )
    for half, cols in halves(width):
        gm_ref[half] = grad_mixed[:, cols]
        decay, gamma = params(par_ref, DECAY, cols), params(par_ref, GAMMA, cols)
        readout = params(par_ref, READ, cols)
        skip = par_ref[SKIP : SKIP + 1, cols]
        passed = [jnp.zeros((SEGS, LANES), F32) for _ in range(2)]
        for i in reversed(range(steps)):
            r = rb_ref[pl.ds(i, SEGS, stride=steps), :]
            g = gm_ref[half, pl.ds(i, SEGS, stride=steps), :]
            for p in range(2):
                passed[p] = (decay[p] * r) * (readout[p] * g + passed[p])
        inits = []
        for p in range(2):
            segw_ref[half, p] = passed[p]
            here = jnp.zeros((1, LANES), F32)
            starts = [here]
            for s in reversed(range(1, SEGS)):
                here = row_of(passed[p], s) + segp_ref[half, p, s : s + 1, :] * here
                starts.append(here)
            tile_ref[1, 2 * p + half : 2 * p + half + 1, :] = (
                row_of(passed[p], 0) + segp_ref[half, p, 0:1, :] * here
            )
            inits.append(jnp.concatenate(starts[::-1], axis=0))
        for i in reversed(range(steps)):
            r = rb_ref[pl.ds(i, SEGS, stride=steps), :]
            g = gm_ref[half, pl.ds(i, SEGS, stride=steps), :]
            total = None
            for p in range(2):
                grad_state = readout[p] * g + inits[p]
                inits[p] = (decay[p] * r) * grad_state
                term = gamma[p] * grad_state
                total = term if total is None else total + term
            gd_ref[pl.ds(i, SEGS, stride=steps), :] = skip * g + total
        halo_ref[:, cols] = gd_ref[0:REACH, :].astype(BF16)
    tile_ref[0] = ends_ref[...]
    for half, cols in halves(width):
        tile_ref[2, half : half + 1, :] = ret_ref[0:1, cols]
    tile_ref[2, 2:4, :] = jnp.ones((2, LANES), F32)
    tile = tile_ref[...]
    for copy in range(pay_ref.shape[0]):
        pay_ref[copy] = tile


def backward_final(
    got_ref, rprod_ref, gm_ref, segw_ref, segp_ref, halo_ref, rb_ref, par_ref, cot_ref,
    out_ref,
    rn_ref, ahead_ref, far_ref, first_ref,
):
    rows, width = cot_ref.shape
    steps = rows // SEGS
    me = lax.axis_index("seq")
    count = rprod_ref.shape[0]
    first_gap, second_gap = dilation(par_ref, 0), dilation(par_ref, 1)
    after = jnp.minimum(me + 1, count - 1)
    for part in range(rows // LANES):
        rn_ref[part * LANES : (part + 1) * LANES, :] = spread_rows(
            got_ref[after, 2, part : part + 1, :]
        )
    whole = decays_of(par_ref, rows)
    arriving = jnp.zeros((4, LANES), F32)
    beyond = jnp.zeros((4, LANES), F32)
    for i in reversed(range(1, count)):
        longer = (whole * rprod_ref[i : i + 1, :]) * arriving + got_ref[i, 1]
        beyond = jnp.where(i > me + 1, longer, beyond)
        arriving = jnp.where(i > me, longer, arriving)
    kept = jnp.ones((SEGS, LANES), F32)
    for i in range(steps):
        kept = kept * rn_ref[pl.ds(i, SEGS, stride=steps), :]
    for half, cols in halves(width):
        decay, gamma = params(par_ref, DECAY, cols), params(par_ref, GAMMA, cols)
        readout = params(par_ref, READ, cols)
        skip = par_ref[SKIP : SKIP + 1, cols]
        here_at, far_at = [], []
        for p in range(2):
            here = row_of(arriving, 2 * p + half)
            far = row_of(beyond, 2 * p + half)
            seg = kept * power(decay[p], steps)
            starts, fars = [here], [far]
            for s in reversed(range(1, SEGS)):
                here = segw_ref[half, p, s : s + 1, :] + segp_ref[half, p, s : s + 1, :] * here
                far = row_of(seg, s) * far
                starts.append(here)
                fars.append(far)
            here_at.append(jnp.concatenate(starts[::-1], axis=0))
            far_at.append(jnp.concatenate(fars[::-1], axis=0))
        for i in reversed(range(steps)):
            r = rb_ref[pl.ds(i, SEGS, stride=steps), :]
            rn = rn_ref[pl.ds(i, SEGS, stride=steps), :]
            g = gm_ref[half, pl.ds(i, SEGS, stride=steps), :]
            total = far_total = None
            for p in range(2):
                grad_state = readout[p] * g + here_at[p]
                here_at[p] = (decay[p] * r) * grad_state
                term = gamma[p] * grad_state
                total = term if total is None else total + term
                term = gamma[p] * far_at[p]
                far_total = term if far_total is None else far_total + term
                far_at[p] = (decay[p] * rn) * far_at[p]
            ahead_ref[pl.ds(i, SEGS, stride=steps), :] = skip * g + total
            far_ref[pl.ds(i, SEGS, stride=steps), :] = far_total
        ahead_ref[rows : rows + REACH, :] = halo_ref[:, cols].astype(F32) + far_ref[0:REACH, :]
        total = jnp.zeros((rows + MARGIN, LANES), F32)
        for k in range(K):
            total = total + par_ref[K + k : K + k + 1, cols] * ahead_ref[
                pl.ds(k * second_gap, rows + MARGIN), :
            ]
        first_ref[...] = total
        total = jnp.zeros((rows, LANES), F32)
        for k in range(K):
            total = total + par_ref[k : k + 1, cols] * first_ref[pl.ds(k * first_gap, rows), :]
        out_ref[:, cols] = (cot_ref[:, cols].astype(F32) + total).astype(BF16)


def near_sum(a_ref, b_ref, c_ref, d_ref, out_ref):
    total = (a_ref[...].astype(F32) + b_ref[...].astype(F32)) + (
        c_ref[...].astype(F32) + d_ref[...].astype(F32)
    )
    rows, width = total.shape
    wide = width // ZSIZE
    for z in range(ZSIZE):
        piece = total[:, z * wide : (z + 1) * wide]
        out_ref[z] = jnp.concatenate([piece[: rows // 2], piece[rows // 2 :]], axis=1).astype(BF16)


def far_sum(in_ref, out_ref):
    total = in_ref[0].astype(F32)
    for z in range(1, ZSIZE):
        total = total + in_ref[z].astype(F32)
    flipped = jnp.transpose(total)
    wide = flipped.shape[0] // 2
    out_ref[...] = jnp.concatenate([flipped[:wide], flipped[wide:]], axis=1)


def vmem(shape, dtype=F32):
    return pltpu.VMEM(shape, dtype)


def call(kernel, outs, scratch=(), smem=(), hbm=(), aliases=None, cost=1):
    def run(*args, after=()):
        used = len(args)
        args = tuple(
            pltpu.with_memory_space_constraint(arg, pltpu.HBM) if i in hbm else arg
            for i, arg in enumerate(args)
        ) + tuple(after)

        def body(*refs):
            kernel(*refs[:used], *refs[len(args) :])

        def space(i):
            return pltpu.SMEM if i in smem else pltpu.HBM if i in hbm else pl.ANY if i >= used else pltpu.VMEM

        return pl.pallas_call(
            body,
            out_shape=tuple(jax.ShapeDtypeStruct(shape, dtype) for shape, dtype in outs),
            in_specs=[pl.BlockSpec(memory_space=space(i)) for i in range(len(args))],
            out_specs=tuple(pl.BlockSpec(memory_space=pltpu.VMEM) for _ in outs),
            scratch_shapes=list(scratch),
            input_output_aliases=aliases or {},
            compiler_params=pltpu.CompilerParams(vmem_limit_bytes=16 * 2**20),
            cost_estimate=pl.CostEstimate(
                flops=0, bytes_accessed=cost * 3_500_000, transcendentals=0
            ),
            name=kernel.__name__,
        )(*args)

    return run


def shifted(block, distance):
    devices = range(lax.axis_size("seq"))
    return lax.ppermute(
        block, "seq", [(i - distance, i) for i in devices if i - distance in devices]
    )


def along_x(block, distance):
    size = XSIZE * ZSIZE
    return lax.ppermute(
        block, "seq", [(i, (i + distance * ZSIZE) % size) for i in range(size)]
    )


def along_y(block, distance):
    size = 2 * YSIZE
    return lax.ppermute(block, "ch", [(i, (i + 2 * distance) % size) for i in range(size)])


def other_core(block):
    return lax.ppermute(block, "ch", [(i, i ^ 1) for i in range(2 * YSIZE)])


def per_device(
    signal, conv_taps, dilations, decays, retention, readout, skip_gain, w_out, cotangent
):
    rows, width = signal.shape
    count = XSIZE * ZSIZE
    nh = width // LANES
    ret = retention.reshape(1, rows)
    skip = skip_gain.reshape(1, width)
    square = (rows, width)
    tall = ((nh, rows, LANES), F32)
    head = ((nh, MARGIN, LANES), F32)
    seg = ((nh, 2, SEGS, LANES), F32)

    halo = shifted(signal[rows - REACH :], 1)
    from_y = [along_y(cotangent, d) for d in range(1, YSIZE)]
    par, rb, driven, fhead, shead, own_cot = call(
        gather_inputs,
        [((PARAMS, width), F32), ((rows, LANES), F32), tall, head, head, (square, BF16)],
        [
            vmem(square, BF16), vmem((2, K, width)), vmem((2, width)), vmem((1, rows)),
            vmem((2, width)), vmem((1, width)), pltpu.SMEM((2,), jnp.int32), vmem((rows, LANES)),
            vmem((rows - MARGIN, LANES)), pltpu.SemaphoreType.DMA((8,)),
        ],
        hbm=range(8), cost=20,
    )(signal, conv_taps, decays, ret, readout, skip, cotangent, dilations)

    driven, ends, segh, segp = call(
        forward_local, [tall, ((4, LANES), F32), seg, seg],
        [vmem((REACH + MARGIN, LANES)), vmem((REACH + MARGIN, LANES))],
        aliases={3: 0}, cost=20,
    )(halo, par, rb, driven, fhead, shead)

    (near,) = call(pack, [((YSIZE,) + square, BF16)])(own_cot, *from_y, after=(segh,))
    far = other_core(near)
    grad_mixed, payload, segw, bhalo = call(
        backward_local, [tall, ((count, 3, 4, LANES), F32), seg, ((REACH, width), BF16)],
        [vmem((rows, LANES)), vmem((3, 4, LANES))], cost=20,
    )(near, far, w_out, segp, par, rb, ends, ret)
    got = lax.all_to_all(payload, "seq", 0, 0, tiled=True)
    later = shifted(bhalo, -1)

    mixed, w0, w1, w2, w3, rprod = call(
        forward_final,
        [(square, BF16)] + [((width, 2 * width), BF16)] * 4 + [((count, LANES), F32)],
        [vmem((nh, rows, LANES))], cost=20,
    )(got, driven, segh, segp, par, rb, near, far, after=(later,))
    w1, w2, w3 = along_x(w1, 1), along_x(w2, 2), along_x(w3, 3)

    (send,) = call(project, [((YSIZE,) + square, BF16)], cost=20)(mixed, w_out)
    pair = other_core(send)
    (grad_signal,) = call(
        backward_final, [(square, BF16)],
        [
            vmem((rows, LANES)), vmem((rows + REACH, LANES)), vmem((rows, LANES)),
            vmem((rows + MARGIN, LANES)),
        ],
        cost=1,
    )(got, rprod, grad_mixed, segw, segp, later, rb, par, own_cot, after=(send,))


    groups = [[x * ZSIZE + z for z in range(ZSIZE)] for x in range(XSIZE)]
    wide = 2 * width // ZSIZE
    (sums,) = call(near_sum, [((ZSIZE, width // 2, 2 * wide), BF16)], cost=20)(
        w0, w1, w2, w3,
        after=(pltpu.with_memory_space_constraint(grad_signal, pltpu.HBM),),
    )
    own, p1, p2, p3 = call(pair_sum, [(square, F32)] + [(square, BF16)] * 3)(
        mixed, w_out, pair, after=(sums,)
    )
    p1, p2, p3 = along_y(p1, 1), along_y(p2, 2), along_y(p3, 3)
    (output,) = call(finish_output, [(square, BF16)])(signal, own, p1, p2, p3)

    sums = lax.all_to_all(sums, "seq", 0, 0, axis_index_groups=groups, tiled=True)
    (grad_w_out,) = call(far_sum, [((wide, width), F32)])(sums)

    return (output, grad_signal, grad_w_out.T)


def solution(mesh):
    return jax.shard_map(
        per_device,
        mesh=mesh,
        in_specs=(
            P("seq", "ch"),
            P(None, None, "ch"),
            P(),
            P(None, "ch"),
            P("seq"),
            P(None, "ch"),
            P("ch"),
            P("ch", None),
            P("seq", "ch"),
        ),
        out_specs=(P("seq", "ch"), P("seq", "ch"), P("ch", "seq")),
        check_vma=False,
    )
```

```python
import jax
import jax.numpy as jnp
from jax import lax
from jax.experimental import pallas as pl
from jax.experimental.pallas import tpu as pltpu
from jax.sharding import PartitionSpec as P

K = 4
DMAX = 16
MARGIN = (K - 1) * DMAX
REACH = 2 * MARGIN
SEGS = 8
LANES = 128
XSIZE, YSIZE, ZSIZE = 4, 4, 8
F32 = jnp.float32
BF16 = jnp.bfloat16
DECAY, GAMMA, READ, SKIP, DIL, KEPT, PARAMS = 8, 10, 12, 14, 15, 16, 24


def spread_rows(row):
    return jnp.transpose(jnp.broadcast_to(row, (LANES, row.shape[1])))


def row_of(value, index):
    return value[index : index + 1]


def power(value, exponent):
    while exponent > 1:
        value = value * value
        exponent //= 2
    return value


def halves(count):
    return [(half, slice(half * LANES, (half + 1) * LANES)) for half in range(count // LANES)]


def params(par_ref, first, cols):
    return [par_ref[first + p : first + p + 1, cols] for p in range(2)]


def dilation(par_ref, which):
    return jnp.max(par_ref[DIL : DIL + 1, which * LANES : (which + 1) * LANES]).astype(jnp.int32)


def x_index():
    return lax.axis_index("seq") // ZSIZE


def y_index():
    return lax.axis_index("ch") // 2


def core_index():
    return lax.rem(lax.axis_index("ch"), 2)


def gather_inputs(
    sig_hbm, taps_hbm, dec_hbm, ret_hbm, ro_hbm, skip_hbm, cot_hbm, dil_hbm,
    par_ref, rb_ref, drv_ref, fhead_ref, shead_ref, cot_ref,
    sig_ref, taps_ref, dec_ref, ret_ref, ro_ref, skip_ref, dil_ref, ext_ref, first_ref, sems,
):
    pairs = (
        (sig_hbm, sig_ref), (taps_hbm, taps_ref), (dec_hbm, dec_ref),
        (ret_hbm, ret_ref), (ro_hbm, ro_ref), (skip_hbm, skip_ref), (cot_hbm, cot_ref),
        (dil_hbm, dil_ref),
    )
    copies = [pltpu.make_async_copy(a, b, sems.at[i]) for i, (a, b) in enumerate(pairs)]
    for copy in copies:
        copy.start()
    for copy in copies:
        copy.wait()
    rows, width = sig_ref.shape
    par_ref[0:K, :] = taps_ref[0]
    par_ref[K : 2 * K, :] = taps_ref[1]
    decays = dec_ref[...]
    par_ref[DECAY : DECAY + 2, :] = decays
    par_ref[GAMMA : GAMMA + 2, :] = jnp.sqrt(1.0 - decays * decays)
    par_ref[READ : READ + 2, :] = ro_ref[...]
    par_ref[SKIP : SKIP + 1, :] = skip_ref[...]
    par_ref[KEPT:PARAMS, :] = jnp.broadcast_to(ret_ref[...], (PARAMS - KEPT, width))
    for which in range(2):
        par_ref[DIL : DIL + 1, which * LANES : (which + 1) * LANES] = jnp.full(
            (1, LANES), dil_ref[which], jnp.int32
        ).astype(F32)
    rb_ref[...] = spread_rows(ret_ref[...])
    for half, cols in halves(width):
        ext_ref[...] = sig_ref[:, cols].astype(F32)
        shead_ref[half] = ext_ref[0:MARGIN, :]
        total = jnp.zeros((rows - MARGIN, LANES), F32)
        for k in range(K):
            total = total + taps_ref[0, k : k + 1, cols] * ext_ref[
                pl.ds(MARGIN - k * dil_ref[0], rows - MARGIN), :
            ]
        first_ref[...] = total
        fhead_ref[half] = first_ref[0:MARGIN, :]
        total = jnp.zeros((rows - REACH, LANES), F32)
        for k in range(K):
            total = total + taps_ref[1, k : k + 1, cols] * first_ref[
                pl.ds(MARGIN - k * dil_ref[1], rows - REACH), :
            ]
        drv_ref[half, 0:REACH, :] = jnp.zeros((REACH, LANES), F32)
        drv_ref[half, REACH:rows, :] = total


def forward_local(
    halo_ref, par_ref, rb_ref, drvin_ref, fhead_ref, shead_ref,
    drv_ref, ends_ref, segh_ref, segp_ref,
    ext_ref, first_ref,
):
    rows = rb_ref.shape[0]
    width = par_ref.shape[1]
    steps = rows // SEGS
    first_gap, second_gap = dilation(par_ref, 0), dilation(par_ref, 1)
    for half, cols in halves(width):
        ext_ref[0:REACH, :] = halo_ref[:, cols].astype(F32)
        ext_ref[REACH : REACH + MARGIN, :] = shead_ref[half]
        total = jnp.zeros((REACH, LANES), F32)
        for k in range(K):
            total = total + par_ref[k : k + 1, cols] * ext_ref[
                pl.ds(MARGIN - k * first_gap, REACH), :
            ]
        first_ref[0:REACH, :] = total
        first_ref[REACH : REACH + MARGIN, :] = fhead_ref[half]
        total = jnp.zeros((REACH, LANES), F32)
        for k in range(K):
            total = total + par_ref[K + k : K + k + 1, cols] * first_ref[
                pl.ds(MARGIN - k * second_gap, REACH), :
            ]
        drv_ref[half, 0:REACH, :] = total
        decay, gamma = params(par_ref, DECAY, cols), params(par_ref, GAMMA, cols)
        state = [jnp.zeros((SEGS, LANES), F32) for _ in range(2)]
        kept = jnp.ones((SEGS, LANES), F32)
        for i in range(steps):
            r = rb_ref[pl.ds(i, SEGS, stride=steps), :]
            u = drv_ref[half, pl.ds(i, SEGS, stride=steps), :]
            kept = kept * r
            for p in range(2):
                state[p] = (decay[p] * r) * state[p] + gamma[p] * u
        for p in range(2):
            seg = kept * power(decay[p], steps)
            segh_ref[half, p] = state[p]
            segp_ref[half, p] = seg
            end = row_of(state[p], 0)
            for s in range(1, SEGS):
                end = row_of(seg, s) * end + row_of(state[p], s)
            ends_ref[2 * p + half : 2 * p + half + 1, :] = end


def decays_of(par_ref, rows):
    parts = [par_ref[DECAY + p : DECAY + p + 1, cols] for p in range(2) for _, cols in halves(2 * LANES)]
    return power(jnp.concatenate(parts, axis=0), rows)


def forward_final(
    got_ref, drv_ref, segh_ref, segp_ref, par_ref, rb_ref,
    mixed_ref, rprod_ref,
    mix_ref,
):
    rows, width = mixed_ref.shape
    steps = rows // SEGS
    me = lax.axis_index("seq")
    count = got_ref.shape[0]
    kept = jnp.concatenate(
        [got_ref[i, 2, 0:1, :] * got_ref[i, 2, 1:2, :] for i in range(count)], axis=0
    )
    gap = LANES // 2
    while gap:
        kept = kept * pltpu.roll(kept, gap, axis=1)
        gap //= 2
    rprod_ref[...] = kept
    whole = decays_of(par_ref, rows)
    entering = jnp.zeros((4, LANES), F32)
    for i in range(count - 1):
        longer = (whole * rprod_ref[i : i + 1, :]) * entering + got_ref[i, 0]
        entering = jnp.where(i < me, longer, entering)
    for half, cols in halves(width):
        decay, gamma = params(par_ref, DECAY, cols), params(par_ref, GAMMA, cols)
        readout = params(par_ref, READ, cols)
        skip = par_ref[SKIP : SKIP + 1, cols]
        state = []
        for p in range(2):
            here = row_of(entering, 2 * p + half)
            starts = [here]
            for s in range(SEGS - 1):
                here = segp_ref[half, p, s : s + 1, :] * here + segh_ref[half, p, s : s + 1, :]
                starts.append(here)
            state.append(jnp.concatenate(starts, axis=0))
        for i in range(steps):
            r = rb_ref[pl.ds(i, SEGS, stride=steps), :]
            u = drv_ref[half, pl.ds(i, SEGS, stride=steps), :]
            for p in range(2):
                state[p] = (decay[p] * r) * state[p] + gamma[p] * u
            mix_ref[half, pl.ds(i, SEGS, stride=steps), :] = (
                readout[0] * state[0] + readout[1] * state[1] + skip * u
            )
        mixed_ref[:, cols] = mix_ref[half].astype(BF16)


def project(mixed_ref, wout_ref, send_ref):
    width = mixed_ref.shape[1]
    for d in range(YSIZE):
        block = 2 * lax.rem(y_index() + d, YSIZE) + 1 - core_index()
        start = pl.multiple_of(block * width, width)
        send_ref[d] = jnp.dot(
            mixed_ref[...], wout_ref[:, pl.ds(start, width)], preferred_element_type=F32
        ).astype(BF16)


def pair_sum(mixed_ref, wout_ref, got_ref, own_ref, a_ref, b_ref, c_ref):
    width = mixed_ref.shape[1]
    for d, out_ref in ((1, a_ref), (2, b_ref), (3, c_ref), (0, own_ref)):
        block = 2 * lax.rem(y_index() + d, YSIZE) + core_index()
        start = pl.multiple_of(block * width, width)
        total = got_ref[d].astype(F32) + jnp.dot(
            mixed_ref[...], wout_ref[:, pl.ds(start, width)], preferred_element_type=F32
        )
        out_ref[...] = total.astype(out_ref.dtype)


def finish_output(sig_ref, own_ref, a_ref, b_ref, c_ref, out_ref):
    total = (own_ref[...] + a_ref[...].astype(F32)) + (
        b_ref[...].astype(F32) + c_ref[...].astype(F32)
    )
    out_ref[...] = (sig_ref[...].astype(F32) + total).astype(BF16)


def facing(distance):
    return lax.rem(y_index() - x_index() - distance + 2 * YSIZE, YSIZE)


def pack(own_ref, a_ref, b_ref, c_ref, out_ref, s1_ref, s2_ref, s3_ref):
    for d, source in enumerate((own_ref, a_ref, b_ref, c_ref)):
        out_ref[d] = source[...]
    for d, send_ref in ((1, s1_ref), (2, s2_ref), (3, s3_ref)):
        send_ref[...] = out_ref[facing(d)]


def stack(near_ref, a_ref, b_ref, c_ref, out_ref):
    width = out_ref.shape[0]
    for d, block in enumerate((near_ref[facing(0)], a_ref[...], b_ref[...], c_ref[...])):
        out_ref[:, d * width : (d + 1) * width] = jnp.transpose(block.astype(F32)).astype(BF16)


def backward_local(
    near_ref, far_ref, wout_ref, segp_ref, par_ref, rb_ref, ends_ref,
    gm_ref, pay_ref,
    tile_ref,
):
    rows = rb_ref.shape[0]
    width = par_ref.shape[1]
    steps = rows // SEGS
    core = core_index()
    grad_mixed = jnp.zeros((rows, width), F32)
    for source, which in ((near_ref, core), (far_ref, 1 - core)):
        for d in range(YSIZE):
            first = 2 * lax.rem(y_index() - d + YSIZE, YSIZE)
            start = pl.multiple_of((first + which) * width, width)
            grad_mixed = grad_mixed + lax.dot_general(
                source[d], wout_ref[:, pl.ds(start, width)], (((1,), (1,)), ((), ())),
                preferred_element_type=F32,
            )
    tile_ref[0] = ends_ref[...]
    tile_ref[2, 2:4, :] = jnp.ones((2, LANES), F32)
    for half, cols in halves(width):
        gm_ref[half, 0:rows, :] = grad_mixed[:, cols]
        tile_ref[2, half : half + 1, :] = par_ref[KEPT : KEPT + 1, cols]
        decay, readout = params(par_ref, DECAY, cols), params(par_ref, READ, cols)
        passed = [jnp.zeros((SEGS, LANES), F32) for _ in range(2)]
        for i in reversed(range(steps)):
            r = rb_ref[pl.ds(i, SEGS, stride=steps), :]
            g = gm_ref[half, pl.ds(i, SEGS, stride=steps), :]
            for p in range(2):
                passed[p] = (decay[p] * r) * (readout[p] * g + passed[p])
        for p in range(2):
            gm_ref[half, rows + p * SEGS : rows + (p + 1) * SEGS, :] = passed[p]
            here = jnp.zeros((1, LANES), F32)
            for s in reversed(range(SEGS)):
                here = row_of(passed[p], s) + segp_ref[half, p, s : s + 1, :] * here
            tile_ref[1, 2 * p + half : 2 * p + half + 1, :] = here
    tile = tile_ref[...]
    for copy in range(pay_ref.shape[0]):
        pay_ref[copy] = tile


def backward_sends(
    gm_ref, segp_ref, par_ref, rb_ref,
    halo_ref,
    gd_ref,
):
    rows = rb_ref.shape[0]
    width = par_ref.shape[1]
    steps = rows // SEGS
    for half, cols in halves(width):
        decay, gamma = params(par_ref, DECAY, cols), params(par_ref, GAMMA, cols)
        readout = params(par_ref, READ, cols)
        skip = par_ref[SKIP : SKIP + 1, cols]
        passed = []
        for p in range(2):
            segw = gm_ref[half, rows + p * SEGS : rows + (p + 1) * SEGS, :]
            here = jnp.zeros((1, LANES), F32)
            starts = [here]
            for s in reversed(range(1, SEGS)):
                here = row_of(segw, s) + segp_ref[half, p, s : s + 1, :] * here
                starts.append(here)
            passed.append(jnp.concatenate(starts[::-1], axis=0))
        for i in reversed(range(steps)):
            r = rb_ref[pl.ds(i, SEGS, stride=steps), :]
            g = gm_ref[half, pl.ds(i, SEGS, stride=steps), :]
            total = None
            for p in range(2):
                grad_state = readout[p] * g + passed[p]
                passed[p] = (decay[p] * r) * grad_state
                term = gamma[p] * grad_state
                total = term if total is None else total + term
            gd_ref[pl.ds(i, SEGS, stride=steps), :] = skip * g + total
        halo_ref[:, cols] = gd_ref[0:REACH, :].astype(BF16)


def backward_final(
    got_ref, rprod_ref, gm_ref, segp_ref, halo_ref, rb_ref, par_ref, cot_ref,
    out_ref,
    rn_ref, ahead_ref, far_ref, first_ref,
):
    rows, width = cot_ref.shape
    steps = rows // SEGS
    me = lax.axis_index("seq")
    count = rprod_ref.shape[0]
    first_gap, second_gap = dilation(par_ref, 0), dilation(par_ref, 1)
    after = jnp.minimum(me + 1, count - 1)
    for part in range(rows // LANES):
        rn_ref[part * LANES : (part + 1) * LANES, :] = spread_rows(
            got_ref[after, 2, part : part + 1, :]
        )
    whole = decays_of(par_ref, rows)
    arriving = jnp.zeros((4, LANES), F32)
    beyond = jnp.zeros((4, LANES), F32)
    for i in reversed(range(1, count)):
        longer = (whole * rprod_ref[i : i + 1, :]) * arriving + got_ref[i, 1]
        beyond = jnp.where(i > me + 1, longer, beyond)
        arriving = jnp.where(i > me, longer, arriving)
    kept = jnp.ones((SEGS, LANES), F32)
    for i in range(steps):
        kept = kept * rn_ref[pl.ds(i, SEGS, stride=steps), :]
    for half, cols in halves(width):
        decay, gamma = params(par_ref, DECAY, cols), params(par_ref, GAMMA, cols)
        readout = params(par_ref, READ, cols)
        skip = par_ref[SKIP : SKIP + 1, cols]
        here_at, far_at = [], []
        for p in range(2):
            here = row_of(arriving, 2 * p + half)
            far = row_of(beyond, 2 * p + half)
            seg = kept * power(decay[p], steps)
            starts, fars = [here], [far]
            for s in reversed(range(1, SEGS)):
                segw = gm_ref[half, rows + p * SEGS + s : rows + p * SEGS + s + 1, :]
                here = segw + segp_ref[half, p, s : s + 1, :] * here
                far = row_of(seg, s) * far
                starts.append(here)
                fars.append(far)
            here_at.append(jnp.concatenate(starts[::-1], axis=0))
            far_at.append(jnp.concatenate(fars[::-1], axis=0))
        for i in reversed(range(steps)):
            r = rb_ref[pl.ds(i, SEGS, stride=steps), :]
            rn = rn_ref[pl.ds(i, SEGS, stride=steps), :]
            g = gm_ref[half, pl.ds(i, SEGS, stride=steps), :]
            total = far_total = None
            for p in range(2):
                grad_state = readout[p] * g + here_at[p]
                here_at[p] = (decay[p] * r) * grad_state
                term = gamma[p] * grad_state
                total = term if total is None else total + term
                term = gamma[p] * far_at[p]
                far_total = term if far_total is None else far_total + term
                far_at[p] = (decay[p] * rn) * far_at[p]
            ahead_ref[pl.ds(i, SEGS, stride=steps), :] = skip * g + total
            far_ref[pl.ds(i, SEGS, stride=steps), :] = far_total
        ahead_ref[rows : rows + REACH, :] = halo_ref[:, cols].astype(F32) + far_ref[0:REACH, :]
        total = jnp.zeros((rows + MARGIN, LANES), F32)
        for k in range(K):
            total = total + par_ref[K + k : K + k + 1, cols] * ahead_ref[
                pl.ds(k * second_gap, rows + MARGIN), :
            ]
        first_ref[...] = total
        total = jnp.zeros((rows, LANES), F32)
        for k in range(K):
            total = total + par_ref[k : k + 1, cols] * first_ref[pl.ds(k * first_gap, rows), :]
        out_ref[:, cols] = (cot_ref[:, cols].astype(F32) + total).astype(BF16)


def weight_pieces(f0_ref, f1_ref, f2_ref, f3_ref, own_ref, other_ref, out_ref):
    mixed = jnp.concatenate([f0_ref[...], f1_ref[...], f2_ref[...], f3_ref[...]], axis=0)
    wide = out_ref.shape[1]
    for source, core in ((own_ref, core_index()), (other_ref, 1 - core_index())):
        total = jnp.dot(source[...], mixed, preferred_element_type=F32).astype(BF16)
        for z in range(ZSIZE // 2):
            out_ref[core * (ZSIZE // 2) + z] = total[z * wide : (z + 1) * wide]


def far_sum(in_ref, out_ref):
    total = in_ref[0].astype(F32)
    for z in range(1, ZSIZE):
        total = total + in_ref[z].astype(F32)
    out_ref[...] = total


def vmem(shape, dtype=F32):
    return pltpu.VMEM(shape, dtype)


def call(kernel, outs, scratch=(), smem=(), hbm=(), aliases=None, cost=1):
    def run(*args, after=()):
        used = len(args)
        args = tuple(
            pltpu.with_memory_space_constraint(arg, pltpu.HBM) if i in hbm else arg
            for i, arg in enumerate(args)
        ) + tuple(after)

        def body(*refs):
            kernel(*refs[:used], *refs[len(args) :])

        def space(i):
            return pltpu.SMEM if i in smem else pltpu.HBM if i in hbm else pl.ANY if i >= used else pltpu.VMEM

        return pl.pallas_call(
            body,
            out_shape=tuple(jax.ShapeDtypeStruct(shape, dtype) for shape, dtype in outs),
            in_specs=[pl.BlockSpec(memory_space=space(i)) for i in range(len(args))],
            out_specs=tuple(pl.BlockSpec(memory_space=pltpu.VMEM) for _ in outs),
            scratch_shapes=list(scratch),
            input_output_aliases=aliases or {},
            compiler_params=pltpu.CompilerParams(vmem_limit_bytes=16 * 2**20),
            cost_estimate=pl.CostEstimate(
                flops=0, bytes_accessed=cost * 3_500_000, transcendentals=0
            ),
            name=kernel.__name__,
        )(*args)

    return run


def shifted(block, distance):
    devices = range(lax.axis_size("seq"))
    return lax.ppermute(
        block, "seq", [(i - distance, i) for i in devices if i - distance in devices]
    )


def along_x(block, distance):
    size = XSIZE * ZSIZE
    return lax.ppermute(
        block, "seq", [(i, (i + distance * ZSIZE) % size) for i in range(size)]
    )


def along_y(block, distance):
    size = 2 * YSIZE
    return lax.ppermute(block, "ch", [(i, (i + 2 * distance) % size) for i in range(size)])


def other_core(block):
    return lax.ppermute(block, "ch", [(i, i ^ 1) for i in range(2 * YSIZE)])


def per_device(
    signal, conv_taps, dilations, decays, retention, readout, skip_gain, w_out, cotangent
):
    rows, width = signal.shape
    count = XSIZE * ZSIZE
    nh = width // LANES
    ret = retention.reshape(1, rows)
    skip = skip_gain.reshape(1, width)
    square = (rows, width)
    tall = ((nh, rows, LANES), F32)
    head = ((nh, MARGIN, LANES), F32)
    seg = ((nh, 2, SEGS, LANES), F32)

    halo = shifted(signal[rows - REACH :], 1)
    from_y = [along_y(cotangent, d) for d in range(1, YSIZE)]
    par, rb, driven, fhead, shead, own_cot = call(
        gather_inputs,
        [((PARAMS, width), F32), ((rows, LANES), F32), tall, head, head, (square, BF16)],
        [
            vmem(square, BF16), vmem((2, K, width)), vmem((2, width)), vmem((1, rows)),
            vmem((2, width)), vmem((1, width)), pltpu.SMEM((2,), jnp.int32), vmem((rows, LANES)),
            vmem((rows - MARGIN, LANES)), pltpu.SemaphoreType.DMA((8,)),
        ],
        hbm=range(8), cost=20,
    )(signal, conv_taps, decays, ret, readout, skip, cotangent, dilations)

    driven, ends, segh, segp = call(
        forward_local, [tall, ((4, LANES), F32), seg, seg],
        [vmem((REACH + MARGIN, LANES)), vmem((REACH + MARGIN, LANES))],
        aliases={3: 0}, cost=20,
    )(halo, par, rb, driven, fhead, shead)

    near, c1, c2, c3 = call(pack, [((YSIZE,) + square, BF16)] + [(square, BF16)] * 3)(
        own_cot, *from_y, after=(segh,)
    )
    c1, c2, c3 = along_x(c1, 1), along_x(c2, 2), along_x(c3, 3)
    far = other_core(near)
    grad_mixed, payload = call(
        backward_local,
        [((nh, rows + 2 * SEGS, LANES), F32), ((count, 3, 4, LANES), F32)],
        [vmem((3, 4, LANES))], cost=20,
    )(near, far, w_out, segp, par, rb, ends)
    got = lax.all_to_all(payload, "seq", 0, 0, tiled=True)

    (chip,) = call(stack, [((width, XSIZE * rows), BF16)])(near, c1, c2, c3, after=(payload,))
    chip_far = other_core(chip)
    (bhalo,) = call(
        backward_sends, [((REACH, width), BF16)], [vmem((rows, LANES))], cost=20,
    )(grad_mixed, segp, par, rb, after=(chip,))
    later = shifted(bhalo, -1)

    mixed, rprod = call(
        forward_final, [(square, BF16), ((count, LANES), F32)],
        [vmem((nh, rows, LANES))], cost=20,
    )(got, driven, segh, segp, par, rb, after=(later, chip))
    f1, f2, f3 = along_x(mixed, 1), along_x(mixed, 2), along_x(mixed, 3)

    (send,) = call(project, [((YSIZE,) + square, BF16)], cost=20)(mixed, w_out)
    pair = other_core(send)

    (grad_signal,) = call(
        backward_final, [(square, BF16)],
        [
            vmem((rows, LANES)), vmem((rows + REACH, LANES)), vmem((rows, LANES)),
            vmem((rows + MARGIN, LANES)),
        ],
        cost=1,
    )(got, rprod, grad_mixed, segp, later, rb, par, own_cot, after=(send,))
    groups = [[x * ZSIZE + z for z in range(ZSIZE)] for x in range(XSIZE)]
    wide = 2 * width // ZSIZE
    (sums,) = call(weight_pieces, [((ZSIZE, wide, width), BF16)], cost=20)(
        mixed, f1, f2, f3, chip, chip_far, after=(pltpu.with_memory_space_constraint(grad_signal, pltpu.HBM),)
    )
    pieces = lax.all_to_all(sums, "seq", 0, 0, axis_index_groups=groups, tiled=True)

    own, p1, p2, p3 = call(pair_sum, [(square, F32)] + [(square, BF16)] * 3)(
        mixed, w_out, pair, after=(sums,)
    )
    p1, p2, p3 = along_y(p1, 1), along_y(p2, 2), along_y(p3, 3)

    (output,) = call(finish_output, [(square, BF16)])(
        signal, own, p1, p2, p3
    )
    (grad_w_out,) = call(far_sum, [((wide, width), F32)])(pieces)
    return (output, grad_signal, grad_w_out.T)


def solution(mesh):
    return jax.shard_map(
        per_device,
        mesh=mesh,
        in_specs=(
            P("seq", "ch"),
            P(None, None, "ch"),
            P(),
            P(None, "ch"),
            P("seq"),
            P(None, "ch"),
            P("ch"),
            P("ch", None),
            P("seq", "ch"),
        ),
        out_specs=(P("seq", "ch"), P("seq", "ch"), P("ch", "seq")),
        check_vma=False,
    )
```

```python
import jax
import jax.numpy as jnp
from jax import lax
from jax.experimental import pallas as pl
from jax.experimental.pallas import tpu as pltpu
from jax.sharding import PartitionSpec as P

K = 4
DMAX = 16
MARGIN = (K - 1) * DMAX
REACH = 2 * MARGIN
SEGS = 8
LANES = 128
XSIZE, YSIZE, ZSIZE = 4, 4, 8
F32 = jnp.float32
BF16 = jnp.bfloat16
DECAY, GAMMA, READ, SKIP, DIL, KEPT, PARAMS = 8, 10, 12, 14, 15, 16, 24


def spread_rows(row):
    return jnp.transpose(jnp.broadcast_to(row, (LANES, row.shape[1])))


def row_of(value, index):
    return value[index : index + 1]


def power(value, exponent):
    while exponent > 1:
        value = value * value
        exponent //= 2
    return value


def halves(count):
    return [(half, slice(half * LANES, (half + 1) * LANES)) for half in range(count // LANES)]


def params(par_ref, first, cols):
    return [par_ref[first + p : first + p + 1, cols] for p in range(2)]


def dilation(par_ref, which):
    return jnp.max(par_ref[DIL : DIL + 1, which * LANES : (which + 1) * LANES]).astype(jnp.int32)


def x_index():
    return lax.axis_index("seq") // ZSIZE


def y_index():
    return lax.axis_index("ch") // 2


def core_index():
    return lax.rem(lax.axis_index("ch"), 2)


def gather_inputs(
    sig_hbm, taps_hbm, dec_hbm, ret_hbm, ro_hbm, skip_hbm, cot_hbm, dil_hbm,
    par_ref, rb_ref, drv_ref, fhead_ref, shead_ref, cot_ref,
    sig_ref, taps_ref, dec_ref, ret_ref, ro_ref, skip_ref, dil_ref, ext_ref, first_ref, sems,
):
    pairs = (
        (sig_hbm, sig_ref), (taps_hbm, taps_ref), (dec_hbm, dec_ref),
        (ret_hbm, ret_ref), (ro_hbm, ro_ref), (skip_hbm, skip_ref), (cot_hbm, cot_ref),
        (dil_hbm, dil_ref),
    )
    copies = [pltpu.make_async_copy(a, b, sems.at[i]) for i, (a, b) in enumerate(pairs)]
    for copy in copies:
        copy.start()
    for copy in copies:
        copy.wait()
    rows, width = sig_ref.shape
    par_ref[0:K, :] = taps_ref[0]
    par_ref[K : 2 * K, :] = taps_ref[1]
    decays = dec_ref[...]
    par_ref[DECAY : DECAY + 2, :] = decays
    par_ref[GAMMA : GAMMA + 2, :] = jnp.sqrt(1.0 - decays * decays)
    par_ref[READ : READ + 2, :] = ro_ref[...]
    par_ref[SKIP : SKIP + 1, :] = skip_ref[...]
    par_ref[KEPT:PARAMS, :] = jnp.broadcast_to(ret_ref[...], (PARAMS - KEPT, width))
    for which in range(2):
        par_ref[DIL : DIL + 1, which * LANES : (which + 1) * LANES] = jnp.full(
            (1, LANES), dil_ref[which], jnp.int32
        ).astype(F32)
    rb_ref[...] = spread_rows(ret_ref[...])
    for half, cols in halves(width):
        ext_ref[...] = sig_ref[:, cols].astype(F32)
        shead_ref[half] = ext_ref[0:MARGIN, :]
        total = jnp.zeros((rows - MARGIN, LANES), F32)
        for k in range(K):
            total = total + taps_ref[0, k : k + 1, cols] * ext_ref[
                pl.ds(MARGIN - k * dil_ref[0], rows - MARGIN), :
            ]
        first_ref[...] = total
        fhead_ref[half] = first_ref[0:MARGIN, :]
        total = jnp.zeros((rows - REACH, LANES), F32)
        for k in range(K):
            total = total + taps_ref[1, k : k + 1, cols] * first_ref[
                pl.ds(MARGIN - k * dil_ref[1], rows - REACH), :
            ]
        drv_ref[half, 0:REACH, :] = jnp.zeros((REACH, LANES), F32)
        drv_ref[half, REACH:rows, :] = total


def forward_local(
    halo_ref, par_ref, rb_ref, drvin_ref, fhead_ref, shead_ref,
    drv_ref, ends_ref, segh_ref, segp_ref,
    ext_ref, first_ref,
):
    rows = rb_ref.shape[0]
    width = par_ref.shape[1]
    steps = rows // SEGS
    first_gap, second_gap = dilation(par_ref, 0), dilation(par_ref, 1)
    for half, cols in halves(width):
        ext_ref[0:REACH, :] = halo_ref[:, cols].astype(F32)
        ext_ref[REACH : REACH + MARGIN, :] = shead_ref[half]
        total = jnp.zeros((REACH, LANES), F32)
        for k in range(K):
            total = total + par_ref[k : k + 1, cols] * ext_ref[
                pl.ds(MARGIN - k * first_gap, REACH), :
            ]
        first_ref[0:REACH, :] = total
        first_ref[REACH : REACH + MARGIN, :] = fhead_ref[half]
        total = jnp.zeros((REACH, LANES), F32)
        for k in range(K):
            total = total + par_ref[K + k : K + k + 1, cols] * first_ref[
                pl.ds(MARGIN - k * second_gap, REACH), :
            ]
        drv_ref[half, 0:REACH, :] = total
        decay, gamma = params(par_ref, DECAY, cols), params(par_ref, GAMMA, cols)
        state = [jnp.zeros((SEGS, LANES), F32) for _ in range(2)]
        kept = jnp.ones((SEGS, LANES), F32)
        for i in range(steps):
            r = rb_ref[pl.ds(i, SEGS, stride=steps), :]
            u = drv_ref[half, pl.ds(i, SEGS, stride=steps), :]
            kept = kept * r
            for p in range(2):
                state[p] = (decay[p] * r) * state[p] + gamma[p] * u
        for p in range(2):
            seg = kept * power(decay[p], steps)
            segh_ref[half, p] = state[p]
            segp_ref[half, p] = seg
            end = row_of(state[p], 0)
            for s in range(1, SEGS):
                end = row_of(seg, s) * end + row_of(state[p], s)
            ends_ref[2 * p + half : 2 * p + half + 1, :] = end


def decays_of(par_ref, rows):
    parts = [par_ref[DECAY + p : DECAY + p + 1, cols] for p in range(2) for _, cols in halves(2 * LANES)]
    return power(jnp.concatenate(parts, axis=0), rows)


def forward_final(
    got_ref, drv_ref, segh_ref, segp_ref, par_ref, rb_ref,
    mixed_ref, rprod_ref,
    mix_ref,
):
    rows, width = mixed_ref.shape
    steps = rows // SEGS
    me = lax.axis_index("seq")
    count = got_ref.shape[0]
    kept = jnp.concatenate(
        [got_ref[i, 2, 0:1, :] * got_ref[i, 2, 1:2, :] for i in range(count)], axis=0
    )
    gap = LANES // 2
    while gap:
        kept = kept * pltpu.roll(kept, gap, axis=1)
        gap //= 2
    rprod_ref[...] = kept
    whole = decays_of(par_ref, rows)
    entering = jnp.zeros((4, LANES), F32)
    for i in range(count - 1):
        longer = (whole * rprod_ref[i : i + 1, :]) * entering + got_ref[i, 0]
        entering = jnp.where(i < me, longer, entering)
    for half, cols in halves(width):
        decay, gamma = params(par_ref, DECAY, cols), params(par_ref, GAMMA, cols)
        readout = params(par_ref, READ, cols)
        skip = par_ref[SKIP : SKIP + 1, cols]
        state = []
        for p in range(2):
            here = row_of(entering, 2 * p + half)
            starts = [here]
            for s in range(SEGS - 1):
                here = segp_ref[half, p, s : s + 1, :] * here + segh_ref[half, p, s : s + 1, :]
                starts.append(here)
            state.append(jnp.concatenate(starts, axis=0))
        for i in range(steps):
            r = rb_ref[pl.ds(i, SEGS, stride=steps), :]
            u = drv_ref[half, pl.ds(i, SEGS, stride=steps), :]
            for p in range(2):
                state[p] = (decay[p] * r) * state[p] + gamma[p] * u
            mix_ref[half, pl.ds(i, SEGS, stride=steps), :] = (
                readout[0] * state[0] + readout[1] * state[1] + skip * u
            )
        mixed_ref[:, cols] = mix_ref[half].astype(BF16)


def project(mixed_ref, wout_ref, send_ref):
    width = mixed_ref.shape[1]
    for d in range(YSIZE):
        block = 2 * lax.rem(y_index() + d, YSIZE) + 1 - core_index()
        start = pl.multiple_of(block * width, width)
        send_ref[d] = jnp.dot(
            mixed_ref[...], wout_ref[:, pl.ds(start, width)], preferred_element_type=F32
        ).astype(BF16)


def pair_sum(mixed_ref, wout_ref, got_ref, own_ref, a_ref, b_ref, c_ref):
    width = mixed_ref.shape[1]
    for d, out_ref in ((1, a_ref), (2, b_ref), (3, c_ref), (0, own_ref)):
        block = 2 * lax.rem(y_index() + d, YSIZE) + core_index()
        start = pl.multiple_of(block * width, width)
        total = got_ref[d].astype(F32) + jnp.dot(
            mixed_ref[...], wout_ref[:, pl.ds(start, width)], preferred_element_type=F32
        )
        out_ref[...] = total.astype(out_ref.dtype)


def finish_output(sig_ref, own_ref, a_ref, b_ref, c_ref, out_ref):
    total = (own_ref[...] + a_ref[...].astype(F32)) + (
        b_ref[...].astype(F32) + c_ref[...].astype(F32)
    )
    out_ref[...] = (sig_ref[...].astype(F32) + total).astype(BF16)


def facing(distance):
    return lax.rem(y_index() - x_index() - distance + 2 * YSIZE, YSIZE)


def pack(own_ref, a_ref, b_ref, c_ref, out_ref, s0_ref, s1_ref, s2_ref, s3_ref):
    for d, source in enumerate((own_ref, a_ref, b_ref, c_ref)):
        out_ref[d] = source[...]
    for d, send_ref in enumerate((s0_ref, s1_ref, s2_ref, s3_ref)):
        send_ref[...] = out_ref[facing(d)]


def stack(own_ref, a_ref, b_ref, c_ref, out_ref):
    width = out_ref.shape[0]
    for d, block in enumerate((own_ref[...], a_ref[...], b_ref[...], c_ref[...])):
        out_ref[:, d * width : (d + 1) * width] = jnp.transpose(block.astype(F32)).astype(BF16)


def backward_local(
    near_ref, far_ref, wout_ref, segp_ref, par_ref, rb_ref, ends_ref,
    gm_ref, pay_ref,
    tile_ref,
):
    rows = rb_ref.shape[0]
    width = par_ref.shape[1]
    steps = rows // SEGS
    core = core_index()
    grad_mixed = jnp.zeros((rows, width), F32)
    for source, which in ((near_ref, core), (far_ref, 1 - core)):
        for d in range(YSIZE):
            first = 2 * lax.rem(y_index() - d + YSIZE, YSIZE)
            start = pl.multiple_of((first + which) * width, width)
            grad_mixed = grad_mixed + lax.dot_general(
                source[d], wout_ref[:, pl.ds(start, width)], (((1,), (1,)), ((), ())),
                preferred_element_type=F32,
            )
    tile_ref[0] = ends_ref[...]
    tile_ref[2, 2:4, :] = jnp.ones((2, LANES), F32)
    for half, cols in halves(width):
        gm_ref[half, 0:rows, :] = grad_mixed[:, cols]
        tile_ref[2, half : half + 1, :] = par_ref[KEPT : KEPT + 1, cols]
        decay, readout = params(par_ref, DECAY, cols), params(par_ref, READ, cols)
        passed = [jnp.zeros((SEGS, LANES), F32) for _ in range(2)]
        for i in reversed(range(steps)):
            r = rb_ref[pl.ds(i, SEGS, stride=steps), :]
            g = gm_ref[half, pl.ds(i, SEGS, stride=steps), :]
            for p in range(2):
                passed[p] = (decay[p] * r) * (readout[p] * g + passed[p])
        for p in range(2):
            gm_ref[half, rows + p * SEGS : rows + (p + 1) * SEGS, :] = passed[p]
            here = jnp.zeros((1, LANES), F32)
            for s in reversed(range(SEGS)):
                here = row_of(passed[p], s) + segp_ref[half, p, s : s + 1, :] * here
            tile_ref[1, 2 * p + half : 2 * p + half + 1, :] = here
    tile = tile_ref[...]
    for copy in range(pay_ref.shape[0]):
        pay_ref[copy] = tile


def backward_sends(
    gm_ref, segp_ref, par_ref, rb_ref,
    halo_ref,
    gd_ref,
):
    rows = rb_ref.shape[0]
    width = par_ref.shape[1]
    steps = rows // SEGS
    for half, cols in halves(width):
        decay, gamma = params(par_ref, DECAY, cols), params(par_ref, GAMMA, cols)
        readout = params(par_ref, READ, cols)
        skip = par_ref[SKIP : SKIP + 1, cols]
        passed = []
        for p in range(2):
            segw = gm_ref[half, rows + p * SEGS : rows + (p + 1) * SEGS, :]
            here = jnp.zeros((1, LANES), F32)
            starts = [here]
            for s in reversed(range(1, SEGS)):
                here = row_of(segw, s) + segp_ref[half, p, s : s + 1, :] * here
                starts.append(here)
            passed.append(jnp.concatenate(starts[::-1], axis=0))
        for i in reversed(range(steps)):
            r = rb_ref[pl.ds(i, SEGS, stride=steps), :]
            g = gm_ref[half, pl.ds(i, SEGS, stride=steps), :]
            total = None
            for p in range(2):
                grad_state = readout[p] * g + passed[p]
                passed[p] = (decay[p] * r) * grad_state
                term = gamma[p] * grad_state
                total = term if total is None else total + term
            gd_ref[pl.ds(i, SEGS, stride=steps), :] = skip * g + total
        halo_ref[:, cols] = gd_ref[0:REACH, :].astype(BF16)


def backward_final(
    got_ref, rprod_ref, gm_ref, segp_ref, halo_ref, rb_ref, par_ref, cot_ref,
    out_ref,
    rn_ref, ahead_ref, far_ref, first_ref,
):
    rows, width = cot_ref.shape
    steps = rows // SEGS
    me = lax.axis_index("seq")
    count = rprod_ref.shape[0]
    first_gap, second_gap = dilation(par_ref, 0), dilation(par_ref, 1)
    after = jnp.minimum(me + 1, count - 1)
    for part in range(rows // LANES):
        rn_ref[part * LANES : (part + 1) * LANES, :] = spread_rows(
            got_ref[after, 2, part : part + 1, :]
        )
    whole = decays_of(par_ref, rows)
    arriving = jnp.zeros((4, LANES), F32)
    beyond = jnp.zeros((4, LANES), F32)
    for i in reversed(range(1, count)):
        longer = (whole * rprod_ref[i : i + 1, :]) * arriving + got_ref[i, 1]
        beyond = jnp.where(i > me + 1, longer, beyond)
        arriving = jnp.where(i > me, longer, arriving)
    kept = jnp.ones((SEGS, LANES), F32)
    for i in range(steps):
        kept = kept * rn_ref[pl.ds(i, SEGS, stride=steps), :]
    for half, cols in halves(width):
        decay, gamma = params(par_ref, DECAY, cols), params(par_ref, GAMMA, cols)
        readout = params(par_ref, READ, cols)
        skip = par_ref[SKIP : SKIP + 1, cols]
        here_at, far_at = [], []
        for p in range(2):
            here = row_of(arriving, 2 * p + half)
            far = row_of(beyond, 2 * p + half)
            seg = kept * power(decay[p], steps)
            starts, fars = [here], [far]
            for s in reversed(range(1, SEGS)):
                segw = gm_ref[half, rows + p * SEGS + s : rows + p * SEGS + s + 1, :]
                here = segw + segp_ref[half, p, s : s + 1, :] * here
                far = row_of(seg, s) * far
                starts.append(here)
                fars.append(far)
            here_at.append(jnp.concatenate(starts[::-1], axis=0))
            far_at.append(jnp.concatenate(fars[::-1], axis=0))
        for i in reversed(range(steps)):
            r = rb_ref[pl.ds(i, SEGS, stride=steps), :]
            rn = rn_ref[pl.ds(i, SEGS, stride=steps), :]
            g = gm_ref[half, pl.ds(i, SEGS, stride=steps), :]
            total = far_total = None
            for p in range(2):
                grad_state = readout[p] * g + here_at[p]
                here_at[p] = (decay[p] * r) * grad_state
                term = gamma[p] * grad_state
                total = term if total is None else total + term
                term = gamma[p] * far_at[p]
                far_total = term if far_total is None else far_total + term
                far_at[p] = (decay[p] * rn) * far_at[p]
            ahead_ref[pl.ds(i, SEGS, stride=steps), :] = skip * g + total
            far_ref[pl.ds(i, SEGS, stride=steps), :] = far_total
        ahead_ref[rows : rows + REACH, :] = halo_ref[:, cols].astype(F32) + far_ref[0:REACH, :]
        total = jnp.zeros((rows + MARGIN, LANES), F32)
        for k in range(K):
            total = total + par_ref[K + k : K + k + 1, cols] * ahead_ref[
                pl.ds(k * second_gap, rows + MARGIN), :
            ]
        first_ref[...] = total
        total = jnp.zeros((rows, LANES), F32)
        for k in range(K):
            total = total + par_ref[k : k + 1, cols] * first_ref[pl.ds(k * first_gap, rows), :]
        out_ref[:, cols] = (cot_ref[:, cols].astype(F32) + total).astype(BF16)


def weight_pieces(f0_ref, f1_ref, f2_ref, f3_ref, own_ref, other_ref, out_ref):
    mixed = jnp.concatenate([f0_ref[...], f1_ref[...], f2_ref[...], f3_ref[...]], axis=0)
    wide = out_ref.shape[1]
    for source, core in ((own_ref, core_index()), (other_ref, 1 - core_index())):
        total = jnp.dot(source[...], mixed, preferred_element_type=F32).astype(BF16)
        for z in range(ZSIZE // 2):
            out_ref[core * (ZSIZE // 2) + z] = total[z * wide : (z + 1) * wide]


def far_sum(in_ref, out_ref):
    total = in_ref[0].astype(F32)
    for z in range(1, ZSIZE):
        total = total + in_ref[z].astype(F32)
    out_ref[...] = total


def vmem(shape, dtype=F32):
    return pltpu.VMEM(shape, dtype)


def call(kernel, outs, scratch=(), smem=(), hbm=(), aliases=None, cost=1):
    def run(*args, after=()):
        used = len(args)
        args = tuple(
            pltpu.with_memory_space_constraint(arg, pltpu.HBM) if i in hbm else arg
            for i, arg in enumerate(args)
        ) + tuple(after)

        def body(*refs):
            kernel(*refs[:used], *refs[len(args) :])

        def space(i):
            return pltpu.SMEM if i in smem else pltpu.HBM if i in hbm else pl.ANY if i >= used else pltpu.VMEM

        return pl.pallas_call(
            body,
            out_shape=tuple(jax.ShapeDtypeStruct(shape, dtype) for shape, dtype in outs),
            in_specs=[pl.BlockSpec(memory_space=space(i)) for i in range(len(args))],
            out_specs=tuple(pl.BlockSpec(memory_space=pltpu.VMEM) for _ in outs),
            scratch_shapes=list(scratch),
            input_output_aliases=aliases or {},
            compiler_params=pltpu.CompilerParams(vmem_limit_bytes=16 * 2**20),
            cost_estimate=pl.CostEstimate(
                flops=0, bytes_accessed=cost * 3_500_000, transcendentals=0
            ),
            name=kernel.__name__,
        )(*args)

    return run


def shifted(block, distance):
    devices = range(lax.axis_size("seq"))
    return lax.ppermute(
        block, "seq", [(i - distance, i) for i in devices if i - distance in devices]
    )


def along_x(block, distance):
    size = XSIZE * ZSIZE
    return lax.ppermute(
        block, "seq", [(i, (i + distance * ZSIZE) % size) for i in range(size)]
    )


def along_y(block, distance):
    size = 2 * YSIZE
    return lax.ppermute(block, "ch", [(i, (i + 2 * distance) % size) for i in range(size)])


def other_core(block):
    return lax.ppermute(block, "ch", [(i, i ^ 1) for i in range(2 * YSIZE)])


def per_device(
    signal, conv_taps, dilations, decays, retention, readout, skip_gain, w_out, cotangent
):
    rows, width = signal.shape
    count = XSIZE * ZSIZE
    nh = width // LANES
    ret = retention.reshape(1, rows)
    skip = skip_gain.reshape(1, width)
    square = (rows, width)
    tall = ((nh, rows, LANES), F32)
    head = ((nh, MARGIN, LANES), F32)
    seg = ((nh, 2, SEGS, LANES), F32)

    halo = shifted(signal[rows - REACH :], 1)
    two, one, three = [along_y(cotangent, d) for d in (2, 1, 3)]
    from_y = [one, two, three]
    par, rb, driven, fhead, shead, own_cot = call(
        gather_inputs,
        [((PARAMS, width), F32), ((rows, LANES), F32), tall, head, head, (square, BF16)],
        [
            vmem(square, BF16), vmem((2, K, width)), vmem((2, width)), vmem((1, rows)),
            vmem((2, width)), vmem((1, width)), pltpu.SMEM((2,), jnp.int32), vmem((rows, LANES)),
            vmem((rows - MARGIN, LANES)), pltpu.SemaphoreType.DMA((8,)),
        ],
        hbm=range(8), cost=20,
    )(signal, conv_taps, decays, ret, readout, skip, cotangent, dilations)

    driven, ends, segh, segp = call(
        forward_local, [tall, ((4, LANES), F32), seg, seg],
        [vmem((REACH + MARGIN, LANES)), vmem((REACH + MARGIN, LANES))],
        aliases={3: 0}, cost=20,
    )(halo, par, rb, driven, fhead, shead)

    near, c0, c1, c2, c3 = call(pack, [((YSIZE,) + square, BF16)] + [(square, BF16)] * 4)(
        own_cot, *from_y, after=(segh,)
    )
    c2, c1, c3 = along_x(c2, 2), along_x(c1, 1), along_x(c3, 3)
    far = other_core(near)
    grad_mixed, payload = call(
        backward_local,
        [((nh, rows + 2 * SEGS, LANES), F32), ((count, 3, 4, LANES), F32)],
        [vmem((3, 4, LANES))], cost=20,
    )(near, far, w_out, segp, par, rb, ends)
    got = lax.all_to_all(payload, "seq", 0, 0, tiled=True)

    (chip,) = call(stack, [((width, XSIZE * rows), BF16)])(c0, c1, c2, c3, after=(payload,))
    chip_far = other_core(chip)
    (bhalo,) = call(
        backward_sends, [((REACH, width), BF16)], [vmem((rows, LANES))], cost=20,
    )(grad_mixed, segp, par, rb, after=(chip,))
    later = shifted(bhalo, -1)

    mixed, rprod = call(
        forward_final, [(square, BF16), ((count, LANES), F32)],
        [vmem((nh, rows, LANES))], cost=20,
    )(got, driven, segh, segp, par, rb, after=(later, chip))
    f2, f1, f3 = along_x(mixed, 2), along_x(mixed, 1), along_x(mixed, 3)

    (send,) = call(project, [((YSIZE,) + square, BF16)], cost=20)(mixed, w_out)
    pair = other_core(send)

    (grad_signal,) = call(
        backward_final, [(square, BF16)],
        [
            vmem((rows, LANES)), vmem((rows + REACH, LANES)), vmem((rows, LANES)),
            vmem((rows + MARGIN, LANES)),
        ],
        cost=1,
    )(got, rprod, grad_mixed, segp, later, rb, par, own_cot, after=(send,))
    groups = [[x * ZSIZE + z for z in range(ZSIZE)] for x in range(XSIZE)]
    wide = 2 * width // ZSIZE
    (sums,) = call(weight_pieces, [((ZSIZE, wide, width), BF16)], cost=20)(
        mixed, f1, f2, f3, chip, chip_far, after=(pltpu.with_memory_space_constraint(grad_signal, pltpu.HBM),)
    )
    pieces = lax.all_to_all(sums, "seq", 0, 0, axis_index_groups=groups, tiled=True)

    own, p1, p2, p3 = call(pair_sum, [(square, F32)] + [(square, BF16)] * 3)(
        mixed, w_out, pair, after=(sums,)
    )
    p2, p1, p3 = along_y(p2, 2), along_y(p1, 1), along_y(p3, 3)

    (output,) = call(finish_output, [(square, BF16)])(
        signal, own, p1, p2, p3
    )
    (grad_w_out,) = call(far_sum, [((wide, width), F32)])(pieces)
    return (output, grad_signal, grad_w_out.T)


def solution(mesh):
    return jax.shard_map(
        per_device,
        mesh=mesh,
        in_specs=(
            P("seq", "ch"),
            P(None, None, "ch"),
            P(),
            P(None, "ch"),
            P("seq"),
            P(None, "ch"),
            P("ch"),
            P("ch", None),
            P("seq", "ch"),
        ),
        out_specs=(P("seq", "ch"), P("seq", "ch"), P("ch", "seq")),
        check_vma=False,
    )
```

```python
import jax
import jax.numpy as jnp
from jax import lax
from jax.experimental import pallas as pl
from jax.experimental.pallas import tpu as pltpu
from jax.sharding import PartitionSpec as P

K = 4
DMAX = 16
MARGIN = (K - 1) * DMAX
REACH = 2 * MARGIN
SEGS = 8
LANES = 128
XSIZE, YSIZE, ZSIZE = 4, 4, 8
F32 = jnp.float32
BF16 = jnp.bfloat16
DECAY, GAMMA, READ, SKIP, DIL, KEPT, PARAMS = 8, 10, 12, 14, 15, 16, 24


def spread_rows(row):
    return jnp.transpose(jnp.broadcast_to(row, (LANES, row.shape[1])))


def row_of(value, index):
    return value[index : index + 1]


def power(value, exponent):
    while exponent > 1:
        value = value * value
        exponent //= 2
    return value


def halves(count):
    return [(half, slice(half * LANES, (half + 1) * LANES)) for half in range(count // LANES)]


def params(par_ref, first, cols):
    return [par_ref[first + p : first + p + 1, cols] for p in range(2)]


def dilation(par_ref, which):
    return jnp.max(par_ref[DIL : DIL + 1, which * LANES : (which + 1) * LANES]).astype(jnp.int32)


def x_index():
    return lax.axis_index("seq") // ZSIZE


def y_index():
    return lax.axis_index("ch") // 2


def core_index():
    return lax.rem(lax.axis_index("ch"), 2)


def gather_inputs(
    sig_hbm, taps_hbm, dec_hbm, ret_hbm, ro_hbm, skip_hbm, cot_hbm, dil_hbm,
    par_ref, rb_ref, drv_ref, fhead_ref, shead_ref, cot_ref,
    sig_ref, taps_ref, dec_ref, ret_ref, ro_ref, skip_ref, dil_ref, ext_ref, first_ref, sems,
):
    pairs = (
        (sig_hbm, sig_ref), (taps_hbm, taps_ref), (dec_hbm, dec_ref),
        (ret_hbm, ret_ref), (ro_hbm, ro_ref), (skip_hbm, skip_ref), (cot_hbm, cot_ref),
        (dil_hbm, dil_ref),
    )
    copies = [pltpu.make_async_copy(a, b, sems.at[i]) for i, (a, b) in enumerate(pairs)]
    for copy in copies:
        copy.start()
    for copy in copies:
        copy.wait()
    rows, width = sig_ref.shape
    par_ref[0:K, :] = taps_ref[0]
    par_ref[K : 2 * K, :] = taps_ref[1]
    decays = dec_ref[...]
    par_ref[DECAY : DECAY + 2, :] = decays
    par_ref[GAMMA : GAMMA + 2, :] = jnp.sqrt(1.0 - decays * decays)
    par_ref[READ : READ + 2, :] = ro_ref[...]
    par_ref[SKIP : SKIP + 1, :] = skip_ref[...]
    par_ref[KEPT:PARAMS, :] = jnp.broadcast_to(ret_ref[...], (PARAMS - KEPT, width))
    for which in range(2):
        par_ref[DIL : DIL + 1, which * LANES : (which + 1) * LANES] = jnp.full(
            (1, LANES), dil_ref[which], jnp.int32
        ).astype(F32)
    rb_ref[...] = spread_rows(ret_ref[...])
    for half, cols in halves(width):
        ext_ref[...] = sig_ref[:, cols].astype(F32)
        shead_ref[half] = ext_ref[0:MARGIN, :]
        total = jnp.zeros((rows - MARGIN, LANES), F32)
        for k in range(K):
            total = total + taps_ref[0, k : k + 1, cols] * ext_ref[
                pl.ds(MARGIN - k * dil_ref[0], rows - MARGIN), :
            ]
        first_ref[...] = total
        fhead_ref[half] = first_ref[0:MARGIN, :]
        total = jnp.zeros((rows - REACH, LANES), F32)
        for k in range(K):
            total = total + taps_ref[1, k : k + 1, cols] * first_ref[
                pl.ds(MARGIN - k * dil_ref[1], rows - REACH), :
            ]
        drv_ref[half, 0:REACH, :] = jnp.zeros((REACH, LANES), F32)
        drv_ref[half, REACH:rows, :] = total


def forward_local(
    halo_ref, par_ref, rb_ref, drvin_ref, fhead_ref, shead_ref,
    drv_ref, ends_ref, segh_ref, segp_ref,
    ext_ref, first_ref,
):
    rows = rb_ref.shape[0]
    width = par_ref.shape[1]
    steps = rows // SEGS
    first_gap, second_gap = dilation(par_ref, 0), dilation(par_ref, 1)
    for half, cols in halves(width):
        ext_ref[0:REACH, :] = halo_ref[:, cols].astype(F32)
        ext_ref[REACH : REACH + MARGIN, :] = shead_ref[half]
        total = jnp.zeros((REACH, LANES), F32)
        for k in range(K):
            total = total + par_ref[k : k + 1, cols] * ext_ref[
                pl.ds(MARGIN - k * first_gap, REACH), :
            ]
        first_ref[0:REACH, :] = total
        first_ref[REACH : REACH + MARGIN, :] = fhead_ref[half]
        total = jnp.zeros((REACH, LANES), F32)
        for k in range(K):
            total = total + par_ref[K + k : K + k + 1, cols] * first_ref[
                pl.ds(MARGIN - k * second_gap, REACH), :
            ]
        drv_ref[half, 0:REACH, :] = total
        decay, gamma = params(par_ref, DECAY, cols), params(par_ref, GAMMA, cols)
        state = [jnp.zeros((SEGS, LANES), F32) for _ in range(2)]
        kept = jnp.ones((SEGS, LANES), F32)
        for i in range(steps):
            r = rb_ref[pl.ds(i, SEGS, stride=steps), :]
            u = drv_ref[half, pl.ds(i, SEGS, stride=steps), :]
            kept = kept * r
            for p in range(2):
                state[p] = (decay[p] * r) * state[p] + gamma[p] * u
        for p in range(2):
            seg = kept * power(decay[p], steps)
            segh_ref[half, p] = state[p]
            segp_ref[half, p] = seg
            end = row_of(state[p], 0)
            for s in range(1, SEGS):
                end = row_of(seg, s) * end + row_of(state[p], s)
            ends_ref[2 * p + half : 2 * p + half + 1, :] = end


def decays_of(par_ref, rows):
    parts = [par_ref[DECAY + p : DECAY + p + 1, cols] for p in range(2) for _, cols in halves(2 * LANES)]
    return power(jnp.concatenate(parts, axis=0), rows)


def forward_final(
    got_ref, drv_ref, segh_ref, segp_ref, par_ref, rb_ref,
    mixed_ref, rprod_ref,
    mix_ref,
):
    rows, width = mixed_ref.shape
    steps = rows // SEGS
    me = lax.axis_index("seq")
    count = got_ref.shape[0]
    kept = jnp.concatenate(
        [got_ref[i, 2, 0:1, :] * got_ref[i, 2, 1:2, :] for i in range(count)], axis=0
    )
    gap = LANES // 2
    while gap:
        kept = kept * pltpu.roll(kept, gap, axis=1)
        gap //= 2
    rprod_ref[...] = kept
    whole = decays_of(par_ref, rows)
    entering = jnp.zeros((4, LANES), F32)
    for i in range(count - 1):
        longer = (whole * rprod_ref[i : i + 1, :]) * entering + got_ref[i, 0]
        entering = jnp.where(i < me, longer, entering)
    for half, cols in halves(width):
        decay, gamma = params(par_ref, DECAY, cols), params(par_ref, GAMMA, cols)
        readout = params(par_ref, READ, cols)
        skip = par_ref[SKIP : SKIP + 1, cols]
        state = []
        for p in range(2):
            here = row_of(entering, 2 * p + half)
            starts = [here]
            for s in range(SEGS - 1):
                here = segp_ref[half, p, s : s + 1, :] * here + segh_ref[half, p, s : s + 1, :]
                starts.append(here)
            state.append(jnp.concatenate(starts, axis=0))
        for i in range(steps):
            r = rb_ref[pl.ds(i, SEGS, stride=steps), :]
            u = drv_ref[half, pl.ds(i, SEGS, stride=steps), :]
            for p in range(2):
                state[p] = (decay[p] * r) * state[p] + gamma[p] * u
            mix_ref[half, pl.ds(i, SEGS, stride=steps), :] = (
                readout[0] * state[0] + readout[1] * state[1] + skip * u
            )
        mixed_ref[:, cols] = mix_ref[half].astype(BF16)


def project(mixed_ref, wout_ref, send_ref):
    width = mixed_ref.shape[1]
    for d in range(YSIZE):
        block = 2 * lax.rem(y_index() + d, YSIZE) + 1 - core_index()
        start = pl.multiple_of(block * width, width)
        send_ref[d] = jnp.dot(
            mixed_ref[...], wout_ref[:, pl.ds(start, width)], preferred_element_type=F32
        ).astype(BF16)


def pair_sum(mixed_ref, wout_ref, got_ref, own_ref, a_ref, b_ref, c_ref):
    width = mixed_ref.shape[1]
    for d, out_ref in ((1, a_ref), (2, b_ref), (3, c_ref), (0, own_ref)):
        block = 2 * lax.rem(y_index() + d, YSIZE) + core_index()
        start = pl.multiple_of(block * width, width)
        total = got_ref[d].astype(F32) + jnp.dot(
            mixed_ref[...], wout_ref[:, pl.ds(start, width)], preferred_element_type=F32
        )
        out_ref[...] = total.astype(out_ref.dtype)


def finish_output(sig_ref, own_ref, a_ref, b_ref, c_ref, out_ref):
    total = (own_ref[...] + a_ref[...].astype(F32)) + (
        b_ref[...].astype(F32) + c_ref[...].astype(F32)
    )
    out_ref[...] = (sig_ref[...].astype(F32) + total).astype(BF16)


def facing(distance):
    return lax.rem(y_index() - x_index() - distance + 2 * YSIZE, YSIZE)


def pack(own_ref, a_ref, b_ref, c_ref, out_ref, s0_ref, s1_ref, s2_ref, s3_ref):
    for d, source in enumerate((own_ref, a_ref, b_ref, c_ref)):
        out_ref[d] = source[...]
    for d, send_ref in enumerate((s0_ref, s1_ref, s2_ref, s3_ref)):
        send_ref[...] = out_ref[facing(d)]


def stack(own_ref, a_ref, b_ref, c_ref, out_ref):
    width = out_ref.shape[0]
    for d, block in enumerate((own_ref[...], a_ref[...], b_ref[...], c_ref[...])):
        out_ref[:, d * width : (d + 1) * width] = jnp.transpose(block.astype(F32)).astype(BF16)


def backward_local(
    near_ref, far_ref, wout_ref, segp_ref, par_ref, rb_ref, ends_ref,
    gm_ref, pay_ref,
    tile_ref,
):
    rows = rb_ref.shape[0]
    width = par_ref.shape[1]
    steps = rows // SEGS
    core = core_index()
    grad_mixed = jnp.zeros((rows, width), F32)
    for source, which in ((near_ref, core), (far_ref, 1 - core)):
        for d in range(YSIZE):
            first = 2 * lax.rem(y_index() - d + YSIZE, YSIZE)
            start = pl.multiple_of((first + which) * width, width)
            grad_mixed = grad_mixed + lax.dot_general(
                source[d], wout_ref[:, pl.ds(start, width)], (((1,), (1,)), ((), ())),
                preferred_element_type=F32,
            )
    tile_ref[0] = ends_ref[...]
    tile_ref[2, 2:4, :] = jnp.ones((2, LANES), F32)
    for half, cols in halves(width):
        gm_ref[half, 0:rows, :] = grad_mixed[:, cols]
        tile_ref[2, half : half + 1, :] = par_ref[KEPT : KEPT + 1, cols]
        decay, readout = params(par_ref, DECAY, cols), params(par_ref, READ, cols)
        passed = [jnp.zeros((SEGS, LANES), F32) for _ in range(2)]
        for i in reversed(range(steps)):
            r = rb_ref[pl.ds(i, SEGS, stride=steps), :]
            g = gm_ref[half, pl.ds(i, SEGS, stride=steps), :]
            for p in range(2):
                passed[p] = (decay[p] * r) * (readout[p] * g + passed[p])
        for p in range(2):
            gm_ref[half, rows + p * SEGS : rows + (p + 1) * SEGS, :] = passed[p]
            here = jnp.zeros((1, LANES), F32)
            for s in reversed(range(SEGS)):
                here = row_of(passed[p], s) + segp_ref[half, p, s : s + 1, :] * here
            tile_ref[1, 2 * p + half : 2 * p + half + 1, :] = here
    tile = tile_ref[...]
    for copy in range(pay_ref.shape[0]):
        pay_ref[copy] = tile


def backward_sends(
    gm_ref, segp_ref, par_ref, rb_ref,
    halo_ref,
    gd_ref,
):
    rows = rb_ref.shape[0]
    width = par_ref.shape[1]
    steps = rows // SEGS
    for half, cols in halves(width):
        decay, gamma = params(par_ref, DECAY, cols), params(par_ref, GAMMA, cols)
        readout = params(par_ref, READ, cols)
        skip = par_ref[SKIP : SKIP + 1, cols]
        passed = []
        for p in range(2):
            segw = gm_ref[half, rows + p * SEGS : rows + (p + 1) * SEGS, :]
            here = jnp.zeros((1, LANES), F32)
            starts = [here]
            for s in reversed(range(1, SEGS)):
                here = row_of(segw, s) + segp_ref[half, p, s : s + 1, :] * here
                starts.append(here)
            passed.append(jnp.concatenate(starts[::-1], axis=0))
        for i in reversed(range(steps)):
            r = rb_ref[pl.ds(i, SEGS, stride=steps), :]
            g = gm_ref[half, pl.ds(i, SEGS, stride=steps), :]
            total = None
            for p in range(2):
                grad_state = readout[p] * g + passed[p]
                passed[p] = (decay[p] * r) * grad_state
                term = gamma[p] * grad_state
                total = term if total is None else total + term
            gd_ref[pl.ds(i, SEGS, stride=steps), :] = skip * g + total
        halo_ref[:, cols] = gd_ref[0:REACH, :].astype(BF16)


def backward_final(
    got_ref, rprod_ref, gm_ref, segp_ref, halo_ref, rb_ref, par_ref, cot_ref,
    out_ref,
    rn_ref, ahead_ref, far_ref, first_ref,
):
    rows, width = cot_ref.shape
    steps = rows // SEGS
    me = lax.axis_index("seq")
    count = rprod_ref.shape[0]
    first_gap, second_gap = dilation(par_ref, 0), dilation(par_ref, 1)
    after = jnp.minimum(me + 1, count - 1)
    for part in range(rows // LANES):
        rn_ref[part * LANES : (part + 1) * LANES, :] = spread_rows(
            got_ref[after, 2, part : part + 1, :]
        )
    whole = decays_of(par_ref, rows)
    arriving = jnp.zeros((4, LANES), F32)
    beyond = jnp.zeros((4, LANES), F32)
    for i in reversed(range(1, count)):
        longer = (whole * rprod_ref[i : i + 1, :]) * arriving + got_ref[i, 1]
        beyond = jnp.where(i > me + 1, longer, beyond)
        arriving = jnp.where(i > me, longer, arriving)
    kept = jnp.ones((SEGS, LANES), F32)
    for i in range(steps):
        kept = kept * rn_ref[pl.ds(i, SEGS, stride=steps), :]
    for half, cols in halves(width):
        decay, gamma = params(par_ref, DECAY, cols), params(par_ref, GAMMA, cols)
        readout = params(par_ref, READ, cols)
        skip = par_ref[SKIP : SKIP + 1, cols]
        here_at, far_at = [], []
        for p in range(2):
            here = row_of(arriving, 2 * p + half)
            far = row_of(beyond, 2 * p + half)
            seg = kept * power(decay[p], steps)
            starts, fars = [here], [far]
            for s in reversed(range(1, SEGS)):
                segw = gm_ref[half, rows + p * SEGS + s : rows + p * SEGS + s + 1, :]
                here = segw + segp_ref[half, p, s : s + 1, :] * here
                far = row_of(seg, s) * far
                starts.append(here)
                fars.append(far)
            here_at.append(jnp.concatenate(starts[::-1], axis=0))
            far_at.append(jnp.concatenate(fars[::-1], axis=0))
        for i in reversed(range(steps)):
            r = rb_ref[pl.ds(i, SEGS, stride=steps), :]
            rn = rn_ref[pl.ds(i, SEGS, stride=steps), :]
            g = gm_ref[half, pl.ds(i, SEGS, stride=steps), :]
            total = far_total = None
            for p in range(2):
                grad_state = readout[p] * g + here_at[p]
                here_at[p] = (decay[p] * r) * grad_state
                term = gamma[p] * grad_state
                total = term if total is None else total + term
                term = gamma[p] * far_at[p]
                far_total = term if far_total is None else far_total + term
                far_at[p] = (decay[p] * rn) * far_at[p]
            ahead_ref[pl.ds(i, SEGS, stride=steps), :] = skip * g + total
            far_ref[pl.ds(i, SEGS, stride=steps), :] = far_total
        ahead_ref[rows : rows + REACH, :] = halo_ref[:, cols].astype(F32) + far_ref[0:REACH, :]
        total = jnp.zeros((rows + MARGIN, LANES), F32)
        for k in range(K):
            total = total + par_ref[K + k : K + k + 1, cols] * ahead_ref[
                pl.ds(k * second_gap, rows + MARGIN), :
            ]
        first_ref[...] = total
        total = jnp.zeros((rows, LANES), F32)
        for k in range(K):
            total = total + par_ref[k : k + 1, cols] * first_ref[pl.ds(k * first_gap, rows), :]
        out_ref[:, cols] = (cot_ref[:, cols].astype(F32) + total).astype(BF16)


def weight_pieces(f0_ref, f1_ref, f2_ref, f3_ref, own_ref, other_ref, out_ref):
    mixed = jnp.concatenate([f0_ref[...], f1_ref[...], f2_ref[...], f3_ref[...]], axis=0)
    wide = out_ref.shape[1]
    for source, core in ((own_ref, core_index()), (other_ref, 1 - core_index())):
        total = jnp.dot(source[...], mixed, preferred_element_type=F32).astype(BF16)
        for z in range(ZSIZE // 2):
            out_ref[core * (ZSIZE // 2) + z] = total[z * wide : (z + 1) * wide]


def far_sum(in_ref, out_ref):
    total = in_ref[0].astype(F32)
    for z in range(1, ZSIZE):
        total = total + in_ref[z].astype(F32)
    out_ref[...] = total


def vmem(shape, dtype=F32):
    return pltpu.VMEM(shape, dtype)


def call(kernel, outs, scratch=(), smem=(), hbm=(), aliases=None, cost=1):
    def run(*args, after=()):
        used = len(args)
        args = tuple(
            pltpu.with_memory_space_constraint(arg, pltpu.HBM) if i in hbm else arg
            for i, arg in enumerate(args)
        ) + tuple(after)

        def body(*refs):
            kernel(*refs[:used], *refs[len(args) :])

        def space(i):
            return pltpu.SMEM if i in smem else pltpu.HBM if i in hbm else pl.ANY if i >= used else pltpu.VMEM

        return pl.pallas_call(
            body,
            out_shape=tuple(jax.ShapeDtypeStruct(shape, dtype) for shape, dtype in outs),
            in_specs=[pl.BlockSpec(memory_space=space(i)) for i in range(len(args))],
            out_specs=tuple(pl.BlockSpec(memory_space=pltpu.VMEM) for _ in outs),
            scratch_shapes=list(scratch),
            input_output_aliases=aliases or {},
            compiler_params=pltpu.CompilerParams(vmem_limit_bytes=16 * 2**20),
            cost_estimate=pl.CostEstimate(
                flops=0, bytes_accessed=cost * 3_500_000, transcendentals=0
            ),
            name=kernel.__name__,
        )(*args)

    return run


def shifted(block, distance):
    devices = range(lax.axis_size("seq"))
    return lax.ppermute(
        block, "seq", [(i - distance, i) for i in devices if i - distance in devices]
    )


def along_x(block, distance):
    size = XSIZE * ZSIZE
    return lax.ppermute(
        block, "seq", [(i, (i + distance * ZSIZE) % size) for i in range(size)]
    )


def along_y(block, distance):
    size = 2 * YSIZE
    return lax.ppermute(block, "ch", [(i, (i + 2 * distance) % size) for i in range(size)])


def other_core(block):
    return lax.ppermute(block, "ch", [(i, i ^ 1) for i in range(2 * YSIZE)])


def per_device(
    signal, conv_taps, dilations, decays, retention, readout, skip_gain, w_out, cotangent
):
    rows, width = signal.shape
    count = XSIZE * ZSIZE
    nh = width // LANES
    ret = retention.reshape(1, rows)
    skip = skip_gain.reshape(1, width)
    square = (rows, width)
    tall = ((nh, rows, LANES), F32)
    head = ((nh, MARGIN, LANES), F32)
    seg = ((nh, 2, SEGS, LANES), F32)

    halo = shifted(signal[rows - REACH :], 1)
    two, one, three = [along_y(cotangent, d) for d in (2, 1, 3)]
    from_y = [one, two, three]
    par, rb, driven, fhead, shead, own_cot = call(
        gather_inputs,
        [((PARAMS, width), F32), ((rows, LANES), F32), tall, head, head, (square, BF16)],
        [
            vmem(square, BF16), vmem((2, K, width)), vmem((2, width)), vmem((1, rows)),
            vmem((2, width)), vmem((1, width)), pltpu.SMEM((2,), jnp.int32), vmem((rows, LANES)),
            vmem((rows - MARGIN, LANES)), pltpu.SemaphoreType.DMA((8,)),
        ],
        hbm=range(8), cost=20,
    )(signal, conv_taps, decays, ret, readout, skip, cotangent, dilations)

    driven, ends, segh, segp = call(
        forward_local, [tall, ((4, LANES), F32), seg, seg],
        [vmem((REACH + MARGIN, LANES)), vmem((REACH + MARGIN, LANES))],
        aliases={3: 0}, cost=20,
    )(halo, par, rb, driven, fhead, shead)

    near, c0, c1, c2, c3 = call(pack, [((YSIZE,) + square, BF16)] + [(square, BF16)] * 4)(
        own_cot, *from_y, after=(segh,)
    )
    c2, c1, c3 = along_x(c2, 2), along_x(c1, 1), along_x(c3, 3)
    far = other_core(near)
    grad_mixed, payload = call(
        backward_local,
        [((nh, rows + 2 * SEGS, LANES), F32), ((count, 3, 4, LANES), F32)],
        [vmem((3, 4, LANES))], cost=20,
    )(near, far, w_out, segp, par, rb, ends)
    got = lax.all_to_all(payload, "seq", 0, 0, tiled=True)

    (chip,) = call(stack, [((width, XSIZE * rows), BF16)])(c0, c1, c2, c3, after=(payload,))
    chip_far = other_core(chip)
    (bhalo,) = call(
        backward_sends, [((REACH, width), BF16)], [vmem((rows, LANES))], cost=20,
    )(grad_mixed, segp, par, rb, after=(chip,))
    later = shifted(bhalo, -1)

    mixed, rprod = call(
        forward_final, [(square, BF16), ((count, LANES), F32)],
        [vmem((nh, rows, LANES))], cost=20,
    )(got, driven, segh, segp, par, rb, after=(later, chip))
    f2, f1, f3 = along_x(mixed, 2), along_x(mixed, 1), along_x(mixed, 3)

    (send,) = call(project, [((YSIZE,) + square, BF16)], cost=20)(mixed, w_out)
    pair = other_core(send)

    (grad_signal,) = call(
        backward_final, [(square, BF16)],
        [
            vmem((rows, LANES)), vmem((rows + REACH, LANES)), vmem((rows, LANES)),
            vmem((rows + MARGIN, LANES)),
        ],
        cost=1,
    )(got, rprod, grad_mixed, segp, later, rb, par, own_cot, after=(send,))
    own, p1, p2, p3 = call(pair_sum, [(square, F32)] + [(square, BF16)] * 3)(
        mixed, w_out, pair,
        after=(pltpu.with_memory_space_constraint(grad_signal, pltpu.HBM),),
    )
    p2, p1, p3 = along_y(p2, 2), along_y(p1, 1), along_y(p3, 3)

    groups = [[x * ZSIZE + z for z in range(ZSIZE)] for x in range(XSIZE)]
    wide = 2 * width // ZSIZE
    (sums,) = call(weight_pieces, [((ZSIZE, wide, width), BF16)], cost=20)(
        mixed, f1, f2, f3, chip, chip_far, after=(own,)
    )
    pieces = lax.all_to_all(sums, "seq", 0, 0, axis_index_groups=groups, tiled=True)

    (output,) = call(finish_output, [(square, BF16)])(
        signal, own, p1, p2, p3
    )
    (grad_w_out,) = call(far_sum, [((wide, width), F32)])(pieces)
    return (output, grad_signal, grad_w_out.T)


def solution(mesh):
    return jax.shard_map(
        per_device,
        mesh=mesh,
        in_specs=(
            P("seq", "ch"),
            P(None, None, "ch"),
            P(),
            P(None, "ch"),
            P("seq"),
            P(None, "ch"),
            P("ch"),
            P("ch", None),
            P("seq", "ch"),
        ),
        out_specs=(P("seq", "ch"), P("seq", "ch"), P("ch", "seq")),
        check_vma=False,
    )
```
